128 devices in a mesh: ctx: 16 (over y, z), tp: 8 (over x, core).
Axes of the slice: x: 4, y: 4, z: 4, core: 2. Of those that a mesh axis runs over, the one named last changes fastest.
Arguments:
- mamba_input: bfloat16 [16384, 16384], P('ctx', 'tp'), may hold values from -6 to 6
- conv_weight: float32 [4, 16384], P(None, 'tp'), may hold values from -3 to 3
- mamba_gate: bfloat16 [16384, 16384], P('ctx', 'tp'), may hold values from -6 to 6
- state_write: bfloat16 [16384, 1024], P('ctx', 'tp'), may hold values from -1 to 1
- state_read: bfloat16 [16384, 1024], P('ctx', 'tp'), may hold values from -6 to 6
- step_size: float32 [256, 16384], P('tp', 'ctx'), may hold values from 0 to 10
- log_decay: float32 [256, 16384], P('tp', 'ctx'), may hold values from -1 to 0
- skip_gain: float32 [256], P('tp'), may hold values from 0.5 to 1.5
- norm_gain: float32 [16384], P('tp'), may hold values from 0.1 to 1.9
Outputs:
- mamba_out: bfloat16 [16384, 16384], P('ctx', 'tp')
The draws below stay inside these ranges and needn't reach their ends.
All inputs are finite; a program needn't handle non-finite values.
Results may differ from the reference program's by a relative error of at most 0.001.
Values may be sent and summed in bfloat16 or wider, within the bound.
No kernel may reach another device: no remote copies, remote signals or barrier semaphores. Data moves between devices by JAX's collectives and lax.ppermute only.
A program may use at most 128 MiB of HBM per device.

```python
import jax
import jax.numpy as jnp
from jax import lax

MHEADS = 256
MDIM = 64
NGROUPS = 8
STATE = 128
CONV = 4
TOK_DEV = 1024
SPAN = 128
SEQ = 16384


def head_law(key, slow_cut, mid_cut):
    ticket = jax.random.randint(jax.random.fold_in(key, 41), (MHEADS, 1), 0, 20)
    slow_rate = jnp.exp(jax.random.uniform(jax.random.fold_in(key, 42), (MHEADS, 1), jnp.float32, jnp.log(0.1 / SEQ), jnp.log(0.6 / SEQ)))
    middle_rate = jnp.exp(jax.random.uniform(jax.random.fold_in(key, 43), (MHEADS, 1), jnp.float32, jnp.log(0.45 / TOK_DEV), jnp.log(1.15 / TOK_DEV)))
    fast_rate = jnp.exp(jax.random.uniform(jax.random.fold_in(key, 44), (MHEADS, 1), jnp.float32, jnp.log(1.0 / 40.0), jnp.log(1.0 / 20.0)))
    slow_heads = ticket < slow_cut
    middle_heads = ticket < mid_cut
    head_rate = jnp.where(slow_heads, slow_rate, jnp.where(middle_heads, middle_rate, fast_rate))
    head_energy = jnp.where(slow_heads, 1.0, jnp.where(middle_heads, 16.0, 8.0))
    step_scale = jnp.sqrt(32.0 * head_energy * jnp.maximum(head_rate, 1.0 / SEQ))
    return (head_rate, step_scale)


def draw_step_size(key, part):
    step_scale = head_law(key, 10, 16)[1]
    key = jax.random.fold_in(key, 7)
    jitter = jax.random.uniform(jax.random.fold_in(key, 1), (MHEADS, SEQ), jnp.float32, 0.5, 1.5)
    return step_scale * jitter


def draw_state_write(key, part):
    key = jax.random.fold_in(key, 9)
    blocks = SEQ // TOK_DEV
    strength = jnp.exp(jax.random.uniform(jax.random.fold_in(key, 1), (blocks, 1, NGROUPS, 1), jnp.float32, jnp.log(0.1), jnp.log(3.0)))
    entries = jnp.clip(jax.random.normal(jax.random.fold_in(key, 2), (blocks, TOK_DEV, NGROUPS, STATE), jnp.float32), -4.0, 4.0)
    return (entries * strength / jnp.sqrt(16.0 * STATE)).reshape(SEQ, NGROUPS * STATE).astype(jnp.bfloat16)


def draw_log_decay(key, part):
    head_rate = head_law(key, 10, 16)[0]
    key = jax.random.fold_in(key, 5)
    device_factor = jnp.exp(jax.random.uniform(jax.random.fold_in(key, 24), (MHEADS, SEQ // TOK_DEV), jnp.float32, jnp.log(0.5), jnp.log(2.0)))
    device_factor = jnp.repeat(device_factor, TOK_DEV, axis=1)
    jitter = jax.random.uniform(jax.random.fold_in(key, 25), (MHEADS, SEQ), jnp.float32, 0.5, 1.5)
    places = jax.random.randint(jax.random.fold_in(key, 26), (3, 1), 1, SEQ)
    struck = jnp.any(jnp.arange(SEQ)[None, :] == places, axis=0)[None, :]
    lost_share = jax.random.uniform(jax.random.fold_in(key, 27), (MHEADS, SEQ), jnp.float32, 0.2, 0.4)
    return -head_rate * device_factor * jitter + jnp.where(struck, jnp.log(1.0 - lost_share), 0.0)


def level_of(key, shape, split, least, top_value):
    level = 1.0
    for dim, parts in split:
        draws = jax.random.uniform(jax.random.fold_in(jax.random.fold_in(key, 6), dim), (parts,), jnp.float32, least / len(split), top_value / len(split))
        level = level * jnp.repeat(jnp.exp(draws), shape[dim] // parts).reshape((-1,) + (1,) * (len(shape) - 1 - dim))
    return level


def normal_values(stream_key, dims, width, bound, split=(), dtype=jnp.bfloat16):
    level = level_of(stream_key, dims, split, -0.22, 0.18) if split else 1.0
    values = jax.random.normal(stream_key, dims, jnp.float32) * width * level
    return jnp.minimum(jnp.maximum(values, -bound), bound).astype(dtype)


def setup_inputs(seed: int = 0) -> dict:
    streams_of = jax.random.split(jax.random.key(seed), 10)
    mamba_input = normal_values(streams_of[0], (SEQ, MHEADS * MDIM), 1.0, 6.0, ((0, 16), (1, 8)))
    conv_weight = normal_values(streams_of[1], (CONV, MHEADS * MDIM), CONV ** -0.5, 3.0, ((1, 8),), jnp.float32)
    mamba_gate = normal_values(streams_of[2], (SEQ, MHEADS * MDIM), 1.0, 6.0, ((0, 16), (1, 8)))
    state_write = draw_state_write(jax.random.fold_in(streams_of[9], 71), 0)
    state_read = normal_values(streams_of[4], (SEQ, NGROUPS * STATE), 1.0, 6.0, ((0, 16), (1, 8)))
    step_size = draw_step_size(jax.random.fold_in(streams_of[9], 71), 0)
    log_decay = draw_log_decay(jax.random.fold_in(streams_of[9], 71), 0)
    skip_gain = jnp.clip(0.5 + 1.0 * jax.random.uniform(streams_of[7], (MHEADS,), jnp.float32) ** level_of(streams_of[7], (MHEADS,), ((0, 8),), -0.2, 0.2), 0.5, 1.5)
    norm_gain = jnp.clip(1.0 + 0.18 * jax.random.normal(streams_of[8], (MHEADS * MDIM,), jnp.float32), 0.1, 1.9)
    return {"mamba_input": mamba_input, "conv_weight": conv_weight, "mamba_gate": mamba_gate, "state_write": state_write, "state_read": state_read, "step_size": step_size, "log_decay": log_decay, "skip_gain": skip_gain, "norm_gain": norm_gain}


def span_step(carried, inputs):
    input_blk, step_blk, decay_blk, write_blk, read_blk = inputs
    length, nheads, hwidth = input_blk.shape
    ngroup = write_blk.shape[1]
    state_dim = write_blk.shape[2]
    per_group = nheads // ngroup
    running = jnp.cumsum(decay_blk, axis=0)
    causal_mask = (lax.iota(jnp.int32, length)[:, None] >= lax.iota(jnp.int32, length)[None, :])[:, :, None]
    decay_gap = jnp.where(causal_mask, running[:, None, :] - running[None, :, :], 0.0)
    fading = jnp.where(causal_mask, jnp.exp(decay_gap), 0.0).reshape(length, length, ngroup, per_group)
    intersection = jnp.einsum('tgn,sgn->tsg', read_blk, write_blk, precision=lax.Precision.HIGHEST)
    scaled = step_blk.reshape(length, ngroup, per_group)
    mixing = fading * intersection[:, :, :, None] * scaled[None, :, :, :]
    input_grp = input_blk.reshape(length, ngroup, per_group, hwidth)
    within = jnp.einsum('tsgh,sghp->tghp', mixing, input_grp, precision=lax.Precision.HIGHEST)
    state_grp = carried.reshape(ngroup, per_group, hwidth, state_dim)
    across = jnp.exp(running).reshape(length, ngroup, per_group)[:, :, :, None] * jnp.einsum('tgn,ghpn->tghp', read_blk, state_grp, precision=lax.Precision.HIGHEST)
    tail_weight = (jnp.exp(running[-1][None, :] - running) * step_blk).reshape(length, ngroup, per_group)
    incoming = jnp.einsum('sgh,sghp,sgn->ghpn', tail_weight, input_grp, write_blk, precision=lax.Precision.HIGHEST)
    new_state = jnp.exp(running[-1])[:, None, None] * carried + incoming.reshape(nheads, hwidth, state_dim)
    return (new_state, (within + across).reshape(length, nheads, hwidth))

def run_spans(input_rows, step_rows, decay_rows, write_rows, read_rows, initial):
    pieces = input_rows.shape[0] // SPAN

    def fold_rows(array):
        return array.reshape((pieces, SPAN) + array.shape[1:])
    final, outputs = lax.scan(span_step, initial, (fold_rows(input_rows), fold_rows(step_rows), fold_rows(decay_rows), fold_rows(write_rows), fold_rows(read_rows)))
    return (final, outputs.reshape(input_rows.shape))

def gated_norm(outputs, input_rows, gate_in, skip_gain, norm_gain, ngroup):
    ssm_total = outputs + skip_gain[None, :, None] * input_rows
    gated = ssm_total * jax.nn.silu(gate_in.astype(jnp.float32).reshape(input_rows.shape))
    token_count = input_rows.shape[0]
    grouped = gated.reshape(token_count, ngroup, -1)
    inverse = lax.rsqrt(lax.optimization_barrier(jnp.mean(grouped * grouped, axis=-1, keepdims=True)) + 1e-05)
    normed = grouped * inverse * norm_gain.reshape(ngroup, -1)[None, :, :]
    return normed.astype(jnp.bfloat16).reshape(token_count, -1)

def causal_conv(mamba_input, conv_weight):
    rows = mamba_input.shape[0]
    padded = jnp.concatenate([jnp.zeros((CONV - 1, mamba_input.shape[1]), jnp.float32), mamba_input.astype(jnp.float32)], axis=0)
    total = jnp.zeros((rows, mamba_input.shape[1]), jnp.float32)
    for tap in range(CONV):
        total = total + conv_weight[tap][None, :] * padded[tap:tap + rows]
    return jax.nn.silu(total)

def reference(mamba_input, conv_weight, mamba_gate, state_write, state_read, step_size, log_decay, skip_gain, norm_gain):
    conv_in = causal_conv(mamba_input, conv_weight)
    input_rows = conv_in.reshape(SEQ, MHEADS, MDIM)
    write_rows = state_write.astype(jnp.float32).reshape(SEQ, NGROUPS, STATE)
    read_rows = state_read.astype(jnp.float32).reshape(SEQ, NGROUPS, STATE)
    initial = jnp.zeros((MHEADS, MDIM, STATE), jnp.float32)
    final, outputs = run_spans(input_rows, step_size.T, log_decay.T, write_rows, read_rows, initial)
    return gated_norm(outputs, input_rows, mamba_gate, skip_gain, norm_gain, NGROUPS)
```

```python
import functools

import jax
import jax.numpy as jnp
from jax import lax
from jax.experimental import pallas as pl
from jax.experimental.pallas import tpu as pltpu
from jax.sharding import PartitionSpec as P

F32 = jnp.float32
BF16 = jnp.bfloat16
HEAD = 64
STATE = 128
TAPS = 4
CHUNK = 128
LANES = 256
EXTRA = 16
HIGHEST = lax.Precision.HIGHEST
VMEM_BYTES = 24 * 1024 * 1024


def iota(shape, dim):
    return lax.broadcasted_iota(jnp.int32, shape, dim)


def dot(a, b):
    return jnp.dot(a, b, preferred_element_type=F32)


def dot_exact(a, b):
    return jnp.dot(a, b, preferred_element_type=F32, precision=HIGHEST)


def split(value):
    high = value.astype(BF16)
    return high, (value - high.astype(F32)).astype(BF16)


def silu_of_half(half):
    return half * jnp.tanh(half) + half


def encode(value):
    top = jnp.max(jnp.abs(value), axis=0, keepdims=True)
    scale = jnp.maximum(top * 1.00390625, 1e-30).astype(BF16).astype(F32)
    size = jnp.exp2(jnp.abs(value) * (252.0 / scale) - 126.0)
    return jnp.where(value < 0, -size, size).astype(BF16), scale


def decode(code, scale):
    code = code.astype(F32)
    size = (jnp.log2(jnp.abs(code)) + 126.0) * (scale * (1.0 / 252.0))
    return jnp.where(code < 0, -size, size)


def stack_chunks(value):
    pieces = value.shape[1] // CHUNK
    return jnp.concatenate([value[:, CHUNK * c : CHUNK * (c + 1)] for c in range(pieces)], axis=0)


def head_spread(heads, channels):
    return (iota((heads, channels), 0) == iota((heads, channels), 1) // HEAD).astype(F32)


def store_tokens(ref, value, heads):
    for c in range(value.shape[0] // heads):
        part = value[heads * c : heads * (c + 1)]
        high = part.astype(BF16).astype(F32)
        both = jnp.concatenate([high, part - high], axis=0)
        ref[CHUNK * c : CHUNK * (c + 1), :] = both.T.astype(BF16)


def conv_half(rows, weight):
    weight = weight * 0.5
    back = pltpu.roll(rows, 1, 0)
    near = rows * weight[3:4] + back * weight[2:3]
    far = rows * weight[1:2] + back * weight[0:1]
    return (near + pltpu.roll(far, 2, 0))[16:]


def end_state_kernel(
    x_ref, weight_ref, write_ref, step_ref, decay_ref, out_ref, gains, spread, keys, parts, packed
):
    heads, tokens = step_ref.shape
    pieces = tokens // CHUNK
    channels = heads * HEAD
    turn = pl.program_id(0)

    @pl.when(turn == 0)
    def prepare():
        decay = decay_ref[...]
        logs = stack_chunks(decay)
        later = (iota((CHUNK, CHUNK), 0) > iota((CHUNK, CHUNK), 1)).astype(F32)
        suffix = dot_exact(logs, later)
        total = suffix[:, 0:1] + logs[:, 0:1]
        offset = jnp.zeros((heads, 1), F32)
        offsets = []
        for c in reversed(range(pieces)):
            offsets.append(offset)
            offset = offset + total[heads * c : heads * (c + 1)]
        suffix = suffix + jnp.concatenate(offsets[::-1], axis=0)
        gain = jnp.exp(suffix) * stack_chunks(step_ref[...])
        row, lane = (iota(gain.shape, 0), iota(gain.shape, 1))
        gain = jnp.where((row < heads) & (lane < TAPS - 1), 0.0, gain)
        store_tokens(gains, gain, heads)
        ones = head_spread(heads, channels)
        spread[...] = jnp.concatenate([ones, ones], axis=0).astype(BF16)
        write_t = write_ref[...].astype(F32).T.astype(BF16)
        keys[...] = jnp.concatenate([write_t, write_t], axis=1)
        first = decay[:, 0:CHUNK]
        lane = iota(first.shape, 1)
        run0 = first[:, 0:1]
        run1 = run0 + first[:, 1:2]
        run2 = run1 + first[:, 2:3]
        step = step_ref[:, 0:CHUNK]
        scalars = jnp.where(lane == 0, jnp.exp(offset), 0.0)
        for t, run in enumerate((run0, run1, run2)):
            scalars = jnp.where(lane == t + 1, jnp.exp(-run) * step[:, t : t + 1], scalars)
        wide = dot_exact(scalars.T[0:8], ones)
        segment = (iota(wide.shape, 1) % HEAD) // (HEAD // 4)
        packed[...] = jnp.broadcast_to(
            jnp.sum(jnp.where(iota(wide.shape, 0) == segment, wide, 0.0), axis=0, keepdims=True),
            packed.shape,
        )

    lanes = pl.ds(pl.multiple_of(turn * LANES, LANES), LANES)
    weight = weight_ref[...]
    for c in range(pieces):
        if c == 0:
            rows = jnp.concatenate([jnp.zeros((16, LANES), BF16), x_ref[0:CHUNK]], axis=0)
        else:
            rows = x_ref[CHUNK * c - 16 : CHUNK * (c + 1)]
        value = silu_of_half(conv_half(rows.astype(F32), weight))
        gain = dot(gains[CHUNK * c : CHUNK * (c + 1)], spread[:, lanes])
        high, low = split(value * gain)
        parts[CHUNK * c : CHUNK * (c + 1)] = high
        parts[tokens + CHUNK * c : tokens + CHUNK * (c + 1)] = low
    state = dot(keys[...], parts[...])
    code, scale = encode(state)
    row = iota((EXTRA, LANES), 0)
    first = pltpu.roll(x_ref[0:16].astype(F32), 7, 0)
    last = pltpu.roll(x_ref[tokens - 16 : tokens].astype(F32), 7, 0)
    writes = pltpu.roll(write_ref[0:16].astype(F32), 1, 0)
    writes = jnp.concatenate([writes] * (LANES // STATE), axis=1)
    scalar = packed[0:1, lanes]
    high = scalar.astype(BF16).astype(F32)
    middle = (scalar - high).astype(BF16).astype(F32)
    low = scalar - high - middle
    extra = jnp.where(row == 0, scale, 0.0)
    extra = jnp.where((row >= 1) & (row <= 3), writes, extra)
    extra = jnp.where((row >= 4) & (row <= 6), last, extra)
    extra = jnp.where((row >= 7) & (row <= 9), first, extra)
    extra = jnp.where(row == 10, high, extra)
    extra = jnp.where(row == 11, middle, extra)
    extra = jnp.where(row == 12, low, extra).astype(BF16)
    for part in range(LANES // 128):
        out_ref[part, 0:STATE] = code[:, 128 * part : 128 * (part + 1)]
        out_ref[part, STATE : STATE + EXTRA] = extra[:, 128 * part : 128 * (part + 1)]


def end_state(x, weight, write, step, decay):
    tokens, channels = x.shape
    heads = step.shape[0]
    owners = channels // 128
    return pl.pallas_call(
        end_state_kernel,
        grid=(channels // LANES,),
        in_specs=[
            pl.BlockSpec((tokens, LANES), lambda j: (0, j)),
            pl.BlockSpec((TAPS, LANES), lambda j: (0, j)),
            pl.BlockSpec((tokens, STATE), lambda j: (0, 0)),
            pl.BlockSpec((heads, tokens), lambda j: (0, 0)),
            pl.BlockSpec((heads, tokens), lambda j: (0, 0)),
        ],
        out_specs=pl.BlockSpec((LANES // 128, STATE + EXTRA, 128), lambda j: (j, 0, 0)),
        out_shape=jax.ShapeDtypeStruct((owners, STATE + EXTRA, 128), BF16),
        scratch_shapes=[
            pltpu.VMEM((tokens, 2 * heads), BF16),
            pltpu.VMEM((2 * heads, channels), BF16),
            pltpu.VMEM((STATE, 2 * tokens), BF16),
            pltpu.VMEM((2 * tokens, LANES), BF16),
            pltpu.VMEM((8, channels), F32),
        ],
        compiler_params=pltpu.CompilerParams(vmem_limit_bytes=VMEM_BYTES),
        name="end_state",
    )(x, weight, write, step, decay)


def prefix_kernel(in_ref, weight_ref, out_ref, blocks):
    count = in_ref.shape[0]
    tile = in_ref[:, STATE : STATE + EXTRA, :].astype(F32)
    shape = tile.shape
    row, lane = (iota(shape, 1), iota(shape, 2))
    before = jnp.concatenate([jnp.zeros((1,) + shape[1:], F32), tile[:-1]], axis=0)
    rows = jnp.where(
        (row >= 4) & (row <= 6), before, jnp.where((row >= 7) & (row <= 9), tile, 0.0)
    )
    weight = weight_ref[...] * 0.5
    half = rows * weight[3:4][None]
    for back in range(1, TAPS):
        half = half + pltpu.roll(rows, back, 1) * weight[3 - back : 4 - back][None]
    value = silu_of_half(half)
    scalars = jnp.sum(jnp.where((row >= 10) & (row <= 12), tile, 0.0), axis=1, keepdims=True)
    left = iota(scalars.shape, 2) < HEAD

    def spread_of(segment):
        place = segment * (HEAD // 4)
        return jnp.where(
            left, scalars[:, :, place : place + 1], scalars[:, :, HEAD + place : HEAD + place + 1]
        )

    fade = spread_of(0)
    gain = jnp.where(row == 7, spread_of(1), jnp.where(row == 8, spread_of(2), spread_of(3)))
    value = jnp.where((row >= 7) & (row <= 9), value * gain, 0.0)
    value = pltpu.roll(value, EXTRA - 6, 1)
    high = value.astype(BF16)
    low = (value - high.astype(F32)).astype(BF16)
    keys = jnp.where((row >= 1) & (row <= 3), tile, 0.0).reshape(count * EXTRA, 128).T.astype(BF16)
    blocks[...] = jnp.zeros(blocks.shape, BF16)
    for j in range(count):
        blocks[EXTRA * j : EXTRA * (j + 1), 128 * j : 128 * (j + 1)] = high[j]
        blocks[EXTRA * (count + j) : EXTRA * (count + j + 1), 128 * j : 128 * (j + 1)] = low[j]
    first = dot(jnp.concatenate([keys, keys], axis=1), blocks[...])
    state = jnp.zeros((STATE, 128), F32)
    zero_rows = jnp.zeros((EXTRA, 128), F32)
    for j in range(count):
        code, scale = encode(state)
        out_ref[j, 0:STATE] = code
        out_ref[j, STATE : STATE + EXTRA] = (zero_rows + scale).astype(BF16)
        local = decode(in_ref[j, 0:STATE], tile[j, 0:1])
        state = fade[j] * (state + first[:, 128 * j : 128 * (j + 1)]) + local


def prefix(received, weight):
    count = received.shape[0]
    whole = pl.BlockSpec(memory_space=pltpu.VMEM)
    return pl.pallas_call(
        prefix_kernel,
        in_specs=[whole, whole],
        out_specs=whole,
        out_shape=jax.ShapeDtypeStruct(received.shape, BF16),
        scratch_shapes=[pltpu.VMEM((2 * count * EXTRA, count * 128), BF16)],
        compiler_params=pltpu.CompilerParams(vmem_limit_bytes=VMEM_BYTES),
        name="prefix",
    )(received, weight)


def local_kernel(
    x_ref,
    halo_ref,
    weight_ref,
    gate_ref,
    write_ref,
    read_ref,
    step_ref,
    decay_ref,
    skip_ref,
    own_ref,
    reach_ref,
    gains,
    fades,
    spread,
    keys,
    mix_a,
    mix_b,
    rowed,
    parts,
):
    heads, tokens = step_ref.shape
    pieces = tokens // CHUNK
    channels = heads * HEAD
    turn = pl.program_id(0)

    @pl.when(turn == 0)
    def prepare():
        logs = stack_chunks(decay_ref[...])
        upto = (iota((CHUNK, CHUNK), 0) <= iota((CHUNK, CHUNK), 1)).astype(F32)
        run = dot_exact(logs, upto)
        middle = run[:, CHUNK // 2 - 1 : CHUNK // 2]
        total = run[:, CHUNK - 1 : CHUNK]
        store_tokens(gains, jnp.exp(middle - run) * stack_chunks(step_ref[...]), heads)
        store_tokens(fades, jnp.exp(run - middle), heads)
        ones = head_spread(heads, channels)
        spread[...] = jnp.concatenate([ones, ones], axis=0).astype(BF16)
        lane = iota((heads, 128), 1)
        scalars = jnp.where(lane == 2 * pieces, skip_ref[...], 0.0)
        offset = jnp.zeros((heads, 1), F32)
        for c in range(pieces):
            mid = middle[heads * c : heads * (c + 1)]
            tot = total[heads * c : heads * (c + 1)]
            scalars = jnp.where(lane == c, jnp.exp(offset + mid), scalars)
            offset = offset + tot
            if c + 1 < pieces:
                onward = jnp.exp(middle[heads * (c + 1) : heads * (c + 2)] + (tot - mid))
                scalars = jnp.where(lane == pieces + c, onward, scalars)
        rowed[...] = dot_exact(scalars.T[0 : rowed.shape[0]], ones)
        causal = iota((CHUNK, CHUNK), 0) >= iota((CHUNK, CHUNK), 1)
        for c in range(pieces):
            span = slice(CHUNK * c, CHUNK * (c + 1))
            write = write_ref[span]
            read = read_ref[span]
            mixing = lax.dot_general(
                read, write, (((1,), (1,)), ((), ())), preferred_element_type=F32
            )
            high, low = split(jnp.where(causal, mixing, 0.0))
            mix_a[span] = jnp.concatenate([high, high], axis=1)
            mix_b[span] = jnp.concatenate([low, read], axis=1)
            write_t = write.astype(F32).T.astype(BF16)
            keys[span] = jnp.concatenate([write_t, write_t], axis=1)

    lanes = pl.ds(pl.multiple_of(turn * LANES, LANES), LANES)
    weight = weight_ref[...]
    skip = rowed[2 * pieces : 2 * pieces + 1, lanes]
    state = jnp.zeros((STATE, LANES), F32)
    for c in range(pieces):
        span = slice(CHUNK * c, CHUNK * (c + 1))
        if c == 0:
            rows = jnp.concatenate([halo_ref[...], x_ref[0:CHUNK]], axis=0)
        else:
            rows = x_ref[CHUNK * c - 16 : CHUNK * (c + 1)]
        value = silu_of_half(conv_half(rows.astype(F32), weight))
        gain = dot(gains[span], spread[:, lanes])
        high, low = split(value * gain)
        parts[0:CHUNK] = high
        parts[CHUNK : 2 * CHUNK] = low
        both = parts[0 : 2 * CHUNK]
        mixed = dot(mix_a[span], both)
        if c == 0:
            mixed = mixed + dot(mix_b[span, 0:CHUNK], high)
        else:
            state_high, state_low = split(state)
            mixed = mixed + dot(mix_b[span], jnp.concatenate([high, state_high], axis=0))
            mixed = mixed + dot(mix_b[span, CHUNK : 2 * CHUNK], state_low)
        if c + 1 < pieces:
            onward = rowed[pieces + c : pieces + c + 1, lanes]
            state = onward * (state + dot(keys[span], both))
        fade = dot(fades[span], spread[:, lanes])
        opened = silu_of_half(gate_ref[span].astype(F32) * 0.5)
        own_ref[span, lanes] = (mixed * fade + skip * value) * opened
        reach_ref[span, lanes] = fade * opened * rowed[c : c + 1, lanes]


def local_part(x, halo, weight, gate, write, read, step, decay, skip):
    tokens, channels = x.shape
    heads = step.shape[0]
    pieces = tokens // CHUNK
    return pl.pallas_call(
        local_kernel,
        grid=(channels // LANES,),
        in_specs=[
            pl.BlockSpec((tokens, LANES), lambda j: (0, j)),
            pl.BlockSpec((16, LANES), lambda j: (0, j)),
            pl.BlockSpec((TAPS, LANES), lambda j: (0, j)),
            pl.BlockSpec((tokens, LANES), lambda j: (0, j)),
            pl.BlockSpec((tokens, STATE), lambda j: (0, 0)),
            pl.BlockSpec((tokens, STATE), lambda j: (0, 0)),
            pl.BlockSpec((heads, tokens), lambda j: (0, 0)),
            pl.BlockSpec((heads, tokens), lambda j: (0, 0)),
            pl.BlockSpec((heads, 1), lambda j: (0, 0)),
        ],
        out_specs=[pl.BlockSpec(memory_space=pltpu.VMEM)] * 2,
        out_shape=[pltpu.VMEM((tokens, channels), F32)] * 2,
        scratch_shapes=[
            pltpu.VMEM((tokens, 2 * heads), BF16),
            pltpu.VMEM((tokens, 2 * heads), BF16),
            pltpu.VMEM((2 * heads, channels), BF16),
            pltpu.VMEM((tokens, 2 * CHUNK), BF16),
            pltpu.VMEM((tokens, 2 * CHUNK), BF16),
            pltpu.VMEM((tokens, 2 * CHUNK), BF16),
            pltpu.VMEM((2 * pieces + 8, channels), F32),
            pltpu.VMEM((2 * CHUNK, LANES), BF16),
        ],
        compiler_params=pltpu.CompilerParams(vmem_limit_bytes=VMEM_BYTES),
        name="local_part",
    )(x, halo, weight, gate, write, read, step, decay, skip)


def final_kernel(state_ref, read_ref, own_ref, reach_ref, gain_ref, out_ref, states, gated):
    owners = state_ref.shape[0]
    turn = pl.program_id(0)
    rows = out_ref.shape[0]
    channels = owners * 128

    @pl.when(turn == 0)
    def prepare():
        for k in range(owners):
            value = decode(state_ref[k, 0:STATE], state_ref[k, STATE : STATE + 1].astype(F32))
            high, low = split(value)
            states[0:STATE, 128 * k : 128 * (k + 1)] = high
            states[STATE : 2 * STATE, 128 * k : 128 * (k + 1)] = low

    read = read_ref[...]
    both = jnp.concatenate([read, read], axis=1)
    start = pl.multiple_of(turn * rows, rows)
    squares = jnp.zeros((rows, 128), F32)
    for j in range(channels // LANES):
        lanes = slice(LANES * j, LANES * (j + 1))
        part = dot(both, states[:, lanes])
        part = own_ref[pl.ds(start, rows), lanes] + reach_ref[pl.ds(start, rows), lanes] * part
        gated[:, lanes] = part
        for i in range(LANES // 128):
            piece = part[:, 128 * i : 128 * (i + 1)]
            squares = squares + piece * piece
    inverse = lax.rsqrt(jnp.sum(squares, axis=1, keepdims=True) * (1.0 / channels) + 1e-05)
    for j in range(channels // LANES):
        lanes = slice(LANES * j, LANES * (j + 1))
        out_ref[:, lanes] = (gated[:, lanes] * inverse * gain_ref[:, lanes]).astype(BF16)


def final_part(entering, read, own, reach, norm_gain):
    tokens, channels = own.shape
    rows = 128
    whole = pl.BlockSpec(memory_space=pltpu.VMEM)
    return pl.pallas_call(
        final_kernel,
        grid=(tokens // rows,),
        in_specs=[
            whole,
            pl.BlockSpec((rows, STATE), lambda i: (i, 0)),
            whole,
            whole,
            pl.BlockSpec((1, channels), lambda i: (0, 0)),
        ],
        out_specs=pl.BlockSpec((rows, channels), lambda i: (i, 0)),
        out_shape=jax.ShapeDtypeStruct((tokens, channels), BF16),
        scratch_shapes=[
            pltpu.VMEM((2 * STATE, channels), BF16),
            pltpu.VMEM((rows, channels), F32),
        ],
        compiler_params=pltpu.CompilerParams(vmem_limit_bytes=VMEM_BYTES),
        name="final_part",
    )(entering, read, own, reach, norm_gain)


def shards(x, weight, gate, write, read, step, decay, skip, norm_gain):
    tokens, channels = x.shape
    count = lax.axis_size("ctx")
    place = lax.axis_index("ctx")
    ends = end_state(x, weight, write, step, decay)
    received = lax.all_to_all(ends, "ctx", 0, 0)
    last, ends = lax.optimization_barrier((x[tokens - 16 :], ends))
    halo = lax.ppermute(last, "ctx", [(i, i + 1) for i in range(count - 1)])
    owned = lax.dynamic_slice(weight, (0, place * 128), (TAPS, 128))
    entering = prefix(received, owned)
    halo, entering = lax.optimization_barrier((halo, entering))
    entering = lax.all_to_all(entering, "ctx", 0, 0)
    own, reach = local_part(x, halo, weight, gate, write, read, step, decay, skip[:, None])
    return final_part(entering, read, own, reach, norm_gain[None, :])


def solution(mesh):
    placed = (
        P("ctx", "tp"),
        P(None, "tp"),
        P("ctx", "tp"),
        P("ctx", "tp"),
        P("ctx", "tp"),
        P("tp", "ctx"),
        P("tp", "ctx"),
        P("tp"),
        P("tp"),
    )
    return jax.shard_map(
        shards, mesh=mesh, in_specs=placed, out_specs=P("ctx", "tp"), check_vma=False
    )
```

```python
import functools

import jax
import jax.numpy as jnp
from jax import lax
from jax.experimental import pallas as pl
from jax.experimental.pallas import tpu as pltpu
from jax.sharding import PartitionSpec as P

F32 = jnp.float32
BF16 = jnp.bfloat16
HEAD = 64
STATE = 128
TAPS = 4
CHUNK = 128
LANES = 256
EXTRA = 16
HIGHEST = lax.Precision.HIGHEST
VMEM_BYTES = 24 * 1024 * 1024


def iota(shape, dim):
    return lax.broadcasted_iota(jnp.int32, shape, dim)


def dot(a, b):
    return jnp.dot(a, b, preferred_element_type=F32)


def dot_exact(a, b):
    return jnp.dot(a, b, preferred_element_type=F32, precision=HIGHEST)


def split(value):
    high = value.astype(BF16)
    return high, (value - high.astype(F32)).astype(BF16)


def silu_of_half(half):
    return half * jnp.tanh(half) + half


def encode(value):
    top = jnp.max(jnp.abs(value), axis=0, keepdims=True)
    scale = jnp.maximum(top * 1.00390625, 1e-30).astype(BF16).astype(F32)
    size = jnp.exp2(jnp.abs(value) * (252.0 / scale) - 126.0)
    return jnp.where(value < 0, -size, size).astype(BF16), scale


def decode(code, scale):
    code = code.astype(F32)
    size = (jnp.log2(jnp.abs(code)) + 126.0) * (scale * (1.0 / 252.0))
    return jnp.where(code < 0, -size, size)


def stack_chunks(value):
    pieces = value.shape[1] // CHUNK
    return jnp.concatenate([value[:, CHUNK * c : CHUNK * (c + 1)] for c in range(pieces)], axis=0)


def head_spread(heads, channels):
    return (iota((heads, channels), 0) == iota((heads, channels), 1) // HEAD).astype(F32)


def store_tokens(ref, value, heads):
    for c in range(value.shape[0] // heads):
        part = value[heads * c : heads * (c + 1)]
        high = part.astype(BF16).astype(F32)
        both = jnp.concatenate([high, part - high], axis=0)
        ref[CHUNK * c : CHUNK * (c + 1), :] = both.T.astype(BF16)


def conv_half(rows, weight):
    weight = weight * 0.5
    back = pltpu.roll(rows, 1, 0)
    near = rows * weight[3:4] + back * weight[2:3]
    far = rows * weight[1:2] + back * weight[0:1]
    return (near + pltpu.roll(far, 2, 0))[16:]


def conv_silu(stage, part, start, count, weight):
    half = stage[part, pl.ds(start + 8, count)] * weight[3:4]
    for back in range(1, TAPS):
        half = half + stage[part, pl.ds(start + 8 - back, count)] * weight[3 - back : 4 - back]
    return silu_of_half(half)


def end_state_kernel(
    x_hbm, weight_hbm, write_hbm, step_hbm, decay_hbm, out_hbm, value_hbm,
    x_ref, weight_ref, write_ref, step_ref, decay_ref, gains, spread, keys, packed, stage, out_ref, value_ref, sems,
):
    heads, tokens = step_ref.shape
    pieces = tokens // CHUNK
    channels = heads * HEAD
    turns = channels // LANES
    small = [
        pltpu.make_async_copy(source, target, sems.at[turns + i])
        for i, (source, target) in enumerate(
            ((decay_hbm, decay_ref), (step_hbm, step_ref), (write_hbm, write_ref), (weight_hbm, weight_ref))
        )
    ]

    def fetch(turn):
        lanes = pl.ds(pl.multiple_of(turn * LANES, LANES), LANES)
        return pltpu.make_async_copy(x_hbm.at[:, lanes], x_ref.at[:, lanes], sems.at[turn])

    def leave(turn):
        lanes = pl.ds(pl.multiple_of(turn * LANES, LANES), LANES)
        return pltpu.make_async_copy(
            value_ref.at[turn], value_hbm.at[:, lanes], sems.at[2 * turns + 4 + turn]
        )

    def leave_code(turn):
        places = pl.ds(turn * (LANES // 128), LANES // 128)
        return pltpu.make_async_copy(out_ref.at[places], out_hbm.at[places], sems.at[turns + 4 + turn])

    for copy in small:
        copy.start()
    for turn in range(turns):
        fetch(turn).start()
    ones = head_spread(heads, channels)
    spread[...] = jnp.concatenate([ones, ones], axis=0).astype(BF16)
    for part in range(LANES // 128):
        stage[part, 0:8] = jnp.zeros((8, 128), F32)
    small[0].wait()
    small[1].wait()
    decay = decay_ref[...]
    logs = stack_chunks(decay)
    later = (iota((CHUNK, CHUNK), 0) > iota((CHUNK, CHUNK), 1)).astype(F32)
    suffix = dot_exact(logs, later)
    total = suffix[:, 0:1] + logs[:, 0:1]
    offset = jnp.zeros((heads, 1), F32)
    offsets = []
    for c in reversed(range(pieces)):
        offsets.append(offset)
        offset = offset + total[heads * c : heads * (c + 1)]
    suffix = suffix + jnp.concatenate(offsets[::-1], axis=0)
    gain = jnp.exp(suffix) * stack_chunks(step_ref[...])
    row, lane = (iota(gain.shape, 0), iota(gain.shape, 1))
    gain = jnp.where((row < heads) & (lane < TAPS - 1), 0.0, gain)
    store_tokens(gains, gain, heads)
    first = decay[:, 0:CHUNK]
    lane = iota(first.shape, 1)
    run0 = first[:, 0:1]
    run1 = run0 + first[:, 1:2]
    run2 = run1 + first[:, 2:3]
    step = step_ref[:, 0:CHUNK]
    scalars = jnp.where(lane == 0, jnp.exp(offset), 0.0)
    for t, run in enumerate((run0, run1, run2)):
        scalars = jnp.where(lane == t + 1, jnp.exp(-run) * step[:, t : t + 1], scalars)
    wide = dot_exact(scalars.T[0:8], ones)
    segment = (iota(wide.shape, 1) % HEAD) // (HEAD // 4)
    packed[...] = jnp.broadcast_to(
        jnp.sum(jnp.where(iota(wide.shape, 0) == segment, wide, 0.0), axis=0, keepdims=True),
        packed.shape,
    )
    small[2].wait()
    small[3].wait()
    write_t = write_ref[...].astype(F32).T.astype(BF16)
    for c in range(pieces):
        part = write_t[:, CHUNK * c : CHUNK * (c + 1)]
        keys[CHUNK * c : CHUNK * (c + 1)] = jnp.concatenate([part, part], axis=1)

    def weigh(turn):
        lanes = pl.ds(pl.multiple_of(turn * LANES, LANES), LANES)
        fetch(turn).wait()
        weight = weight_ref[:, lanes] * 0.5
        state = jnp.zeros((STATE, LANES), F32)
        for c in range(pieces):
            span = slice(CHUNK * c, CHUNK * (c + 1))
            rows = x_ref[span, lanes].astype(F32)
            gain = dot(gains[span], spread[:, lanes])
            sides = []
            for part in range(LANES // 128):
                cols = slice(128 * part, 128 * (part + 1))
                stage[part, 8 + CHUNK * c : 8 + CHUNK * (c + 1)] = rows[:, cols]
                value = conv_silu(stage, part, CHUNK * c, CHUNK, weight[:, cols])
                value_ref[turn, span, cols] = value
                sides.append(jnp.concatenate(split(value * gain[:, cols]), axis=0))
            state = state + dot(keys[span], jnp.concatenate(sides, axis=1))
        leave(turn).start()
        return state

    def finish(turn, state):
        lanes = pl.ds(pl.multiple_of(turn * LANES, LANES), LANES)
        code, scale = encode(state)
        row = iota((EXTRA, LANES), 0)
        first = pltpu.roll(x_ref[0:16, lanes].astype(F32), 7, 0)
        last = pltpu.roll(x_ref[tokens - 16 : tokens, lanes].astype(F32), 7, 0)
        writes = pltpu.roll(write_ref[0:16].astype(F32), 1, 0)
        writes = jnp.concatenate([writes] * (LANES // STATE), axis=1)
        scalar = packed[0:1, lanes]
        high = scalar.astype(BF16).astype(F32)
        middle = (scalar - high).astype(BF16).astype(F32)
        low = scalar - high - middle
        extra = jnp.where(row == 0, scale, 0.0)
        extra = jnp.where((row >= 1) & (row <= 3), writes, extra)
        extra = jnp.where((row >= 4) & (row <= 6), last, extra)
        extra = jnp.where((row >= 7) & (row <= 9), first, extra)
        extra = jnp.where(row == 10, high, extra)
        extra = jnp.where(row == 11, middle, extra)
        extra = jnp.where(row == 12, low, extra).astype(BF16)
        for part in range(LANES // 128):
            place = turn * (LANES // 128) + part
            out_ref[place, 0:STATE] = code[:, 128 * part : 128 * (part + 1)]
            out_ref[place, STATE : STATE + EXTRA] = extra[:, 128 * part : 128 * (part + 1)]

    def pair(i, carry):
        for side in range(2):
            turn = 2 * i + side
            finish(turn, weigh(turn))
            leave_code(turn).start()
        return carry

    lax.fori_loop(0, turns // 2, pair, 0)
    for turn in range(turns):
        leave(turn).wait()
        leave_code(turn).wait()


def in_hbm(*values):
    return [pltpu.with_memory_space_constraint(value, pltpu.HBM) for value in values]


def end_state(x, weight, write, step, decay):
    tokens, channels = x.shape
    heads = step.shape[0]
    owners = channels // 128
    return pl.pallas_call(
        end_state_kernel,
        in_specs=[pl.BlockSpec(memory_space=pltpu.HBM)] * 5,
        out_specs=[pl.BlockSpec(memory_space=pltpu.HBM)] * 2,
        out_shape=[pltpu.HBM((owners, STATE + EXTRA, 128), BF16), pltpu.HBM((tokens, channels), F32)],
        scratch_shapes=[
            pltpu.VMEM(x.shape, BF16),
            pltpu.VMEM(weight.shape, F32),
            pltpu.VMEM(write.shape, BF16),
            pltpu.VMEM(step.shape, F32),
            pltpu.VMEM(decay.shape, F32),
            pltpu.VMEM((tokens, 2 * heads), BF16),
            pltpu.VMEM((2 * heads, channels), BF16),
            pltpu.VMEM((tokens, 2 * CHUNK), BF16),
            pltpu.VMEM((8, channels), F32),
            pltpu.VMEM((LANES // 128, 8 + tokens, 128), F32),
            pltpu.VMEM((owners, STATE + EXTRA, 128), BF16),
            pltpu.VMEM((channels // LANES, tokens, LANES), F32),
            pltpu.SemaphoreType.DMA((3 * (channels // LANES) + 4,)),
        ],
        compiler_params=pltpu.CompilerParams(vmem_limit_bytes=VMEM_BYTES),
        name="end_state",
    )(*in_hbm(x, weight, write, step, decay))


def prefix_kernel(place_ref, in_ref, weight_ref, out_ref, blocks):
    count = in_ref.shape[0]
    tile = in_ref[:, STATE : STATE + EXTRA, :].astype(F32)
    shape = tile.shape
    row, lane = (iota(shape, 1), iota(shape, 2))
    before = jnp.concatenate([jnp.zeros((1,) + shape[1:], F32), tile[:-1]], axis=0)
    rows = jnp.where(
        (row >= 4) & (row <= 6), before, jnp.where((row >= 7) & (row <= 9), tile, 0.0)
    )
    weight = weight_ref[:, pl.ds(pl.multiple_of(place_ref[0] * 128, 128), 128)] * 0.5
    half = rows * weight[3:4][None]
    for back in range(1, TAPS):
        half = half + pltpu.roll(rows, back, 1) * weight[3 - back : 4 - back][None]
    value = silu_of_half(half)
    scalars = jnp.sum(jnp.where((row >= 10) & (row <= 12), tile, 0.0), axis=1, keepdims=True)
    left = iota(scalars.shape, 2) < HEAD

    def spread_of(segment):
        place = segment * (HEAD // 4)
        return jnp.where(
            left, scalars[:, :, place : place + 1], scalars[:, :, HEAD + place : HEAD + place + 1]
        )

    fade = spread_of(0)
    gain = jnp.where(row == 7, spread_of(1), jnp.where(row == 8, spread_of(2), spread_of(3)))
    coarse = value.astype(BF16).astype(F32)
    firsts = jnp.where(row <= 3, pltpu.roll(coarse, EXTRA - 6, 1), pltpu.roll(value - coarse, EXTRA - 3, 1))
    value = jnp.where((row >= 7) & (row <= 9), value * gain, 0.0)
    value = pltpu.roll(value, EXTRA - 6, 1)
    high = value.astype(BF16)
    low = (value - high.astype(F32)).astype(BF16)
    keys = jnp.where((row >= 1) & (row <= 3), tile, 0.0).reshape(count * EXTRA, 128).T.astype(BF16)
    blocks[...] = jnp.zeros(blocks.shape, BF16)
    for j in range(count):
        blocks[EXTRA * j : EXTRA * (j + 1), 128 * j : 128 * (j + 1)] = high[j]
        blocks[EXTRA * (count + j) : EXTRA * (count + j + 1), 128 * j : 128 * (j + 1)] = low[j]
    first = dot(jnp.concatenate([keys, keys], axis=1), blocks[...])
    state = jnp.zeros((STATE, 128), F32)
    top_row = iota((EXTRA, 128), 0) == 0
    for j in range(count):
        state = state + first[:, 128 * j : 128 * (j + 1)]
        code, scale = encode(state)
        out_ref[j, 0:STATE] = code
        out_ref[j, STATE : STATE + EXTRA] = jnp.where(top_row, scale, firsts[j]).astype(BF16)
        local = decode(in_ref[j, 0:STATE], tile[j, 0:1])
        state = fade[j] * state + local


def prefix(place, received, weight):
    count = received.shape[0]
    whole = pl.BlockSpec(memory_space=pltpu.VMEM)
    return pl.pallas_call(
        prefix_kernel,
        in_specs=[pl.BlockSpec(memory_space=pltpu.SMEM), whole, whole],
        out_specs=whole,
        out_shape=jax.ShapeDtypeStruct(received.shape, BF16),
        scratch_shapes=[pltpu.VMEM((2 * count * EXTRA, count * 128), BF16)],
        compiler_params=pltpu.CompilerParams(vmem_limit_bytes=VMEM_BYTES),
        name="prefix",
    )(place, received, weight)


def local_tables_kernel(
    write_hbm, read_hbm, step_hbm, decay_hbm, skip_ref, gains_out, fades_out, reach_out, keys_out, mix_out, rowed_out,
    write_ref, read_ref, step_ref, decay_ref, gains, fades, reach, keys, mix, rowed, sems,
):
    heads, tokens = step_ref.shape
    pieces = tokens // CHUNK
    channels = heads * HEAD
    moves = [
        pltpu.make_async_copy(source, target, sems.at[i])
        for i, (source, target) in enumerate(
            (
                (decay_hbm, decay_ref), (step_hbm, step_ref), (write_hbm, write_ref), (read_hbm, read_ref),
                (gains, gains_out), (fades, fades_out), (reach, reach_out), (keys, keys_out), (mix, mix_out),
                (rowed, rowed_out),
            )
        )
    ]
    for copy in moves[:4]:
        copy.start()
    ones = head_spread(heads, channels)
    for copy in moves[:4]:
        copy.wait()
    logs = stack_chunks(decay_ref[...])
    upto = (iota((CHUNK, CHUNK), 0) <= iota((CHUNK, CHUNK), 1)).astype(F32)
    run = dot_exact(logs, upto)
    middle = run[:, CHUNK // 2 - 1 : CHUNK // 2]
    total = run[:, CHUNK - 1 : CHUNK]
    gain = jnp.exp(middle - run) * stack_chunks(step_ref[...])
    gain = jnp.where((iota(gain.shape, 0) < heads) & (iota(gain.shape, 1) < TAPS - 1), 0.0, gain)
    store_tokens(gains, gain, heads)
    store_tokens(fades, jnp.exp(run - middle), heads)
    lane = iota((heads, 128), 1)
    scalars = jnp.where(lane == pieces, skip_ref[...], 0.0)
    offset = jnp.zeros((heads, 1), F32)
    offsets = []
    for c in range(pieces):
        offsets.append(offset)
        mid = middle[heads * c : heads * (c + 1)]
        tot = total[heads * c : heads * (c + 1)]
        offset = offset + tot
        if c + 1 < pieces:
            onward = jnp.exp(middle[heads * (c + 1) : heads * (c + 2)] + (tot - mid))
            scalars = jnp.where(lane == c, onward, scalars)
    store_tokens(reach, jnp.exp(run + jnp.concatenate(offsets, axis=0)), heads)
    causal = iota((CHUNK, CHUNK), 0) >= iota((CHUNK, CHUNK), 1)
    for c in range(pieces):
        span = slice(CHUNK * c, CHUNK * (c + 1))
        write = write_ref[span]
        read = read_ref[span]
        mixing = lax.dot_general(read, write, (((1,), (1,)), ((), ())), preferred_element_type=F32)
        if c == 0:
            place = pieces + 1
            for t, later in ((0, 1), (0, 2), (1, 2)):
                weight = jnp.exp(run[0:heads, t : t + 1] - run[0:heads, later : later + 1])
                weight = weight * step_ref[:, later : later + 1] * mixing[t : t + 1, later : later + 1]
                scalars = jnp.where(lane == place, weight, scalars)
                place += 1
        high, low = split(jnp.where(causal, mixing, 0.0))
        mix[span] = jnp.concatenate([high, high, low, read, read], axis=1)
        write_t = write.astype(F32).T.astype(BF16)
        keys[span] = jnp.concatenate([write_t, write_t], axis=1)
    rowed[...] = dot_exact(scalars.T[0 : rowed.shape[0]], ones)
    for copy in moves[4:]:
        copy.start()
    for copy in moves[4:]:
        copy.wait()


def local_tables(write, read, step, decay, skip):
    heads, tokens = step.shape
    pieces = tokens // CHUNK
    channels = heads * HEAD
    hbm = pl.BlockSpec(memory_space=pltpu.HBM)
    outs = [
        ((tokens, 2 * heads), BF16),
        ((tokens, 2 * heads), BF16),
        ((tokens, 2 * heads), BF16),
        ((tokens, 2 * CHUNK), BF16),
        ((tokens, 5 * CHUNK), BF16),
        ((pieces + 8, channels), F32),
    ]
    ins = (write, read, step, decay)
    return pl.pallas_call(
        local_tables_kernel,
        in_specs=[hbm] * 4 + [pl.BlockSpec(memory_space=pltpu.VMEM)],
        out_specs=[hbm] * len(outs),
        out_shape=[pltpu.HBM(*out) for out in outs],
        scratch_shapes=[pltpu.VMEM(value.shape, value.dtype) for value in ins]
        + [pltpu.VMEM(*out) for out in outs]
        + [pltpu.SemaphoreType.DMA((len(ins) + len(outs),))],
        compiler_params=pltpu.CompilerParams(vmem_limit_bytes=VMEM_BYTES),
        name="local_tables",
    )(*in_hbm(*ins), skip)


def local_kernel(
    begin, value_hbm, gains_hbm, fades_hbm, keys_hbm, mix_hbm, rowed_hbm, local_hbm,
    value_ref, gains, fades, keys, mix, rowed, spread, gain0, gain1, fade0, fade1, result, sems,
):
    tokens, width = local_hbm.shape
    pieces = tokens // CHUNK
    channels = rowed.shape[1]
    turns = width // LANES
    wide_gains, wide_fades = (gain0, gain1), (fade0, fade1)
    pairs = (
        (gains_hbm, gains), (keys_hbm, keys), (mix_hbm, mix), (rowed_hbm, rowed), (fades_hbm, fades)
    )
    small = [
        pltpu.make_async_copy(source, target, sems.at[2 * turns + i])
        for i, (source, target) in enumerate(pairs)
    ]

    def columns(turn):
        return pl.ds(pl.multiple_of(turn * LANES, LANES), LANES)

    def fetch(turn):
        return pltpu.make_async_copy(
            value_hbm.at[:, columns(turn + begin)], value_ref.at[turn], sems.at[turn]
        )

    def leave(turn):
        return pltpu.make_async_copy(
            result.at[turn], local_hbm.at[:, columns(turn)], sems.at[turns + turn]
        )

    def widen(turn, side):
        lanes = columns(turn + begin)
        wide_gains[side][...] = dot(gains[...], spread[:, lanes])
        wide_fades[side][...] = dot(fades[...], spread[:, lanes])

    small[0].start()
    fetch(0).start()
    for copy in small[1:]:
        copy.start()
    for turn in range(1, turns):
        fetch(turn).start()
    ones = head_spread(channels // HEAD, channels)
    spread[...] = jnp.concatenate([ones, ones], axis=0).astype(BF16)
    for copy in small:
        copy.wait()
    widen(0, 0)

    def work(turn, side):
        lanes = columns(turn + begin)
        fetch(turn).wait()
        skip = rowed[pieces : pieces + 1, lanes]
        widen(jnp.minimum(turn + 1, turns - 1), 1 - side)
        state = None
        for c in range(pieces):
            span = slice(CHUNK * c, CHUNK * (c + 1))
            both = jnp.concatenate(split(value_ref[turn, span] * wide_gains[side][span]), axis=0)
            if state is None:
                mixed = dot(mix[span, 0 : 3 * CHUNK], jnp.concatenate([both, both[0:CHUNK]], axis=0))
                state = dot(keys[span], both)
            else:
                high, low = split(state)
                mixed = dot(mix[span], jnp.concatenate([both, both[0:CHUNK], high, low], axis=0))
                if c + 1 < pieces:
                    state = state + dot(keys[span], both)
            if c + 1 < pieces:
                state = state * rowed[c : c + 1, lanes]
            result[turn, span] = mixed * wide_fades[side][span] + skip * value_ref[turn, span]
        leave(turn).start()

    def pair(i, carry):
        for side in range(2):
            work(2 * i + side, side)
        return carry

    lax.fori_loop(0, turns // 2, pair, 0)
    for turn in range(turns):
        leave(turn).wait()


def local_part(begin, turns, value, gains, fades, keys, mix, rowed):
    tokens, channels = value.shape
    hbm = pl.BlockSpec(memory_space=pltpu.HBM)
    inputs = in_hbm(value, gains, fades, keys, mix, rowed)
    return pl.pallas_call(
        functools.partial(local_kernel, begin),
        in_specs=[hbm] * 6,
        out_specs=hbm,
        out_shape=pltpu.HBM((tokens, turns * LANES), F32),
        scratch_shapes=[
            pltpu.VMEM((turns, tokens, LANES), F32),
            pltpu.VMEM(gains.shape, BF16),
            pltpu.VMEM(fades.shape, BF16),
            pltpu.VMEM(keys.shape, BF16),
            pltpu.VMEM(mix.shape, BF16),
            pltpu.VMEM(rowed.shape, F32),
            pltpu.VMEM((2 * (channels // HEAD), channels), BF16),
            pltpu.VMEM((tokens, LANES), F32),
            pltpu.VMEM((tokens, LANES), F32),
            pltpu.VMEM((tokens, LANES), F32),
            pltpu.VMEM((tokens, LANES), F32),
            pltpu.VMEM((turns, tokens, LANES), F32),
            pltpu.SemaphoreType.DMA((2 * turns + 5,)),
        ],
        compiler_params=pltpu.CompilerParams(vmem_limit_bytes=VMEM_BYTES),
        name="local_part",
    )(*inputs)


def final_kernel(
    state_ref, gain_ref, read_hbm, fade_hbm, rowed_hbm, left_hbm, right_hbm, gate_hbm, out_hbm,
    read_ref, fade_ref, rowed, local_ref, gate_ref, states, spread, gated, out_ref, sems,
):
    owners = state_ref.shape[0]
    channels = owners * 128
    tokens = read_ref.shape[0]
    heads = channels // HEAD
    turns = tokens // CHUNK

    def rows(turn):
        return pl.ds(pl.multiple_of(turn * CHUNK, CHUNK), CHUNK)

    def fetch(turn):
        half = left_hbm.shape[1]
        moves = (
            (left_hbm.at[rows(turn)], local_ref.at[rows(turn), 0:half]),
            (right_hbm.at[rows(turn)], local_ref.at[rows(turn), half:channels]),
            (gate_hbm.at[rows(turn)], gate_ref.at[rows(turn)]),
        )
        return [
            pltpu.make_async_copy(source, target, sems.at[i, turn])
            for i, (source, target) in enumerate(moves)
        ]

    def leave(turn):
        return pltpu.make_async_copy(out_ref.at[rows(turn)], out_hbm.at[rows(turn)], sems.at[4, turn])

    small = [
        pltpu.make_async_copy(read_hbm, read_ref, sems.at[3, 2]),
        pltpu.make_async_copy(fade_hbm, fade_ref, sems.at[3, 3]),
        pltpu.make_async_copy(rowed_hbm, rowed, sems.at[3, 4]),
    ]
    for copy in small:
        copy.start()
    for turn in range(turns):
        for copy in fetch(turn):
            copy.start()
    ones = head_spread(heads, channels)
    spread[...] = jnp.concatenate([ones, ones], axis=0).astype(BF16)
    for k in range(owners):
        value = decode(state_ref[k, 0:STATE], state_ref[k, STATE : STATE + 1].astype(F32))
        high, low = split(value)
        states[0:STATE, 128 * k : 128 * (k + 1)] = high
        states[STATE : 2 * STATE, 128 * k : 128 * (k + 1)] = low
    for copy in small:
        copy.wait()
    for copy in fetch(0):
        copy.wait()
    pieces = tokens // CHUNK
    row = iota((8, 128), 0)
    for k in range(owners):
        lanes = slice(128 * k, 128 * (k + 1))
        firsts = state_ref[k, STATE : STATE + EXTRA].astype(F32)
        value0, value1, value2 = (firsts[t : t + 1] + firsts[t + 3 : t + 4] for t in (1, 2, 3))
        skip, mix01, mix02, mix12 = (rowed[pieces + i : pieces + i + 1, lanes] for i in range(4))
        patch = jnp.where(row == 2, skip * value2, local_ref[0:8, lanes])
        patch = jnp.where(row == 1, skip * value1 - mix12 * value2, patch)
        patch = jnp.where(row == 0, skip * value0 - mix01 * value1 - mix02 * value2, patch)
        local_ref[0:8, lanes] = patch

    def work(turn):
        span = rows(turn)
        read = read_ref[span]
        both = jnp.concatenate([read, read], axis=1)
        fade = fade_ref[span]
        squares = jnp.zeros((CHUNK, 128), F32)
        for j in range(channels // LANES):
            lanes = slice(LANES * j, LANES * (j + 1))
            reach = dot(both, states[:, lanes]) * dot(fade, spread[:, lanes])
            opened = silu_of_half(gate_ref[span, lanes].astype(F32) * 0.5)
            part = (local_ref[span, lanes] + reach) * opened
            gated[:, lanes] = part
            for i in range(LANES // 128):
                piece = part[:, 128 * i : 128 * (i + 1)]
                squares = squares + piece * piece
        inverse = lax.rsqrt(jnp.sum(squares, axis=1, keepdims=True) * (1.0 / channels) + 1e-05)
        for j in range(channels // LANES):
            lanes = slice(LANES * j, LANES * (j + 1))
            out_ref[span, lanes] = (gated[:, lanes] * inverse * gain_ref[:, lanes]).astype(BF16)
        leave(turn).start()

    work(0)

    def later(turn, carry):
        for copy in fetch(turn):
            copy.wait()
        work(turn)
        return carry

    lax.fori_loop(1, turns, later, 0)
    for turn in range(turns):
        leave(turn).wait()


def final_part(entering, norm_gain, read, fade, rowed, left, right, gate):
    tokens, channels = gate.shape
    heads = channels // HEAD
    hbm = pl.BlockSpec(memory_space=pltpu.HBM)
    vmem = pl.BlockSpec(memory_space=pltpu.VMEM)
    return pl.pallas_call(
        final_kernel,
        in_specs=[vmem] * 2 + [hbm] * 6,
        out_specs=hbm,
        out_shape=pltpu.HBM((tokens, channels), BF16),
        scratch_shapes=[
            pltpu.VMEM(read.shape, BF16),
            pltpu.VMEM(fade.shape, BF16),
            pltpu.VMEM(rowed.shape, F32),
            pltpu.VMEM((tokens, channels), F32),
            pltpu.VMEM(gate.shape, BF16),
            pltpu.VMEM((2 * STATE, channels), BF16),
            pltpu.VMEM((2 * heads, channels), BF16),
            pltpu.VMEM((CHUNK, channels), F32),
            pltpu.VMEM((tokens, channels), BF16),
            pltpu.SemaphoreType.DMA((5, tokens // CHUNK)),
        ],
        compiler_params=pltpu.CompilerParams(vmem_limit_bytes=VMEM_BYTES),
        name="final_part",
    )(entering, norm_gain, *in_hbm(read, fade, rowed, left, right, gate))


def shards(x, weight, gate, write, read, step, decay, skip, norm_gain):
    place = lax.axis_index("ctx")
    turns = x.shape[1] // LANES
    ends, value = end_state(x, weight, write, step, decay)
    received = lax.all_to_all(ends, "ctx", 0, 0)
    decay, ends = lax.optimization_barrier((decay, ends))
    gains, fades, reach, keys, mix, rowed = local_tables(write, read, step, decay, skip[:, None])
    part = turns // 4
    left = local_part(0, part, value, gains, fades, keys, mix, rowed)
    received, left = lax.optimization_barrier((received, left))
    entering = prefix(place[None], received, weight)
    value, entering = lax.optimization_barrier((value, entering))
    entering = lax.all_to_all(entering, "ctx", 0, 0)
    right = local_part(part, turns - part, value, gains, fades, keys, mix, rowed)
    return final_part(entering, norm_gain[None, :], read, reach, rowed, left, right, gate)


def solution(mesh):
    placed = (
        P("ctx", "tp"),
        P(None, "tp"),
        P("ctx", "tp"),
        P("ctx", "tp"),
        P("ctx", "tp"),
        P("tp", "ctx"),
        P("tp", "ctx"),
        P("tp"),
        P("tp"),
    )
    return jax.shard_map(
        shards, mesh=mesh, in_specs=placed, out_specs=P("ctx", "tp"), check_vma=False
    )
```

```python
import functools

import jax
import jax.numpy as jnp
from jax import lax
from jax.experimental import pallas as pl
from jax.experimental.pallas import tpu as pltpu
from jax.sharding import PartitionSpec as P

F32 = jnp.float32
BF16 = jnp.bfloat16
HEAD = 64
STATE = 128
TAPS = 4
CHUNK = 128
LANES = 256
EXTRA = 16
VMEM_BYTES = 24 * 1024 * 1024


def iota(shape, dim):
    return lax.broadcasted_iota(jnp.int32, shape, dim)


def dot(a, b):
    return jnp.dot(a, b, preferred_element_type=F32)


def dot_binary(a, b):
    high = a.astype(BF16)
    rest = a - high.astype(F32)
    middle = rest.astype(BF16)
    low = (rest - middle.astype(F32)).astype(BF16)
    b = b.astype(BF16)
    return dot(jnp.concatenate([high, middle, low], axis=1), jnp.concatenate([b, b, b], axis=0))


def split(value):
    high = value.astype(BF16)
    return high, (value - high.astype(F32)).astype(BF16)


def silu_of_half(half):
    return half * jnp.tanh(half) + half


def encode(value):
    top = jnp.max(jnp.abs(value), axis=0, keepdims=True)
    scale = jnp.maximum(top * 1.00390625, 1e-30).astype(BF16).astype(F32)
    return jnp.exp2(value * (126.0 / scale)).astype(BF16), scale


def decode(code, scale):
    return jnp.log2(code.astype(F32)) * (scale * (1.0 / 126.0))


def stack_chunks(value):
    pieces = value.shape[1] // CHUNK
    return jnp.concatenate([value[:, CHUNK * c : CHUNK * (c + 1)] for c in range(pieces)], axis=0)


def head_spread(heads, channels):
    return (iota((heads, channels), 0) == iota((heads, channels), 1) // HEAD).astype(F32)


def store_tokens(ref, value, heads):
    for c in range(value.shape[0] // heads):
        part = value[heads * c : heads * (c + 1)]
        high = part.astype(BF16).astype(F32)
        both = jnp.concatenate([high, part - high], axis=0)
        ref[CHUNK * c : CHUNK * (c + 1), :] = both.T.astype(BF16)


def conv_half(rows, weight):
    weight = weight * 0.5
    back = pltpu.roll(rows, 1, 0)
    near = rows * weight[3:4] + back * weight[2:3]
    far = rows * weight[1:2] + back * weight[0:1]
    return (near + pltpu.roll(far, 2, 0))[16:]


def conv_silu(stage, part, start, count, weight):
    half = stage[part, pl.ds(start + 8, count)] * weight[3:4]
    for back in range(1, TAPS):
        half = half + stage[part, pl.ds(start + 8 - back, count)] * weight[3 - back : 4 - back]
    return silu_of_half(half)


def end_state_kernel(
    x_hbm, weight_hbm, write_hbm, step_hbm, decay_hbm, out_hbm, value_hbm,
    x_ref, weight_ref, write_ref, step_ref, decay_ref, gains, spread, keys, packed, stage, out_ref, value_ref, sems,
):
    heads, tokens = step_ref.shape
    pieces = tokens // CHUNK
    channels = heads * HEAD
    turns = channels // LANES
    small = [
        pltpu.make_async_copy(source, target, sems.at[turns + i])
        for i, (source, target) in enumerate(
            ((decay_hbm, decay_ref), (step_hbm, step_ref), (write_hbm, write_ref), (weight_hbm, weight_ref))
        )
    ]

    def fetch(turn):
        lanes = pl.ds(pl.multiple_of(turn * LANES, LANES), LANES)
        return pltpu.make_async_copy(x_hbm.at[:, lanes], x_ref.at[:, lanes], sems.at[turn])

    def leave(turn):
        lanes = pl.ds(pl.multiple_of(turn * LANES, LANES), LANES)
        return pltpu.make_async_copy(
            value_ref.at[turn], value_hbm.at[:, lanes], sems.at[2 * turns + 4 + turn]
        )

    def leave_code(turn):
        places = pl.ds(turn * (LANES // 128), LANES // 128)
        return pltpu.make_async_copy(out_ref.at[places], out_hbm.at[places], sems.at[turns + 4 + turn])

    for copy in small:
        copy.start()
    for turn in range(turns):
        fetch(turn).start()
    ones = head_spread(heads, channels)
    spread[...] = jnp.concatenate([ones, ones], axis=0).astype(BF16)
    for part in range(LANES // 128):
        stage[part, 0:8] = jnp.zeros((8, 128), F32)
    small[0].wait()
    small[1].wait()
    decay = decay_ref[...]
    logs = stack_chunks(decay)
    later = (iota((CHUNK, CHUNK), 0) > iota((CHUNK, CHUNK), 1)).astype(F32)
    suffix = dot_binary(logs, later)
    total = suffix[:, 0:1] + logs[:, 0:1]
    offset = jnp.zeros((heads, 1), F32)
    offsets = []
    for c in reversed(range(pieces)):
        offsets.append(offset)
        offset = offset + total[heads * c : heads * (c + 1)]
    suffix = suffix + jnp.concatenate(offsets[::-1], axis=0)
    gain = jnp.exp(suffix) * stack_chunks(step_ref[...])
    row, lane = (iota(gain.shape, 0), iota(gain.shape, 1))
    gain = jnp.where((row < heads) & (lane < TAPS - 1), 0.0, gain)
    store_tokens(gains, gain, heads)
    first = decay[:, 0:CHUNK]
    lane = iota(first.shape, 1)
    run0 = first[:, 0:1]
    run1 = run0 + first[:, 1:2]
    run2 = run1 + first[:, 2:3]
    step = step_ref[:, 0:CHUNK]
    scalars = jnp.where(lane == 0, jnp.exp(offset), 0.0)
    for t, run in enumerate((run0, run1, run2)):
        scalars = jnp.where(lane == t + 1, jnp.exp(-run) * step[:, t : t + 1], scalars)
    wide = dot_binary(scalars.T[0:8], ones)
    segment = (iota(wide.shape, 1) % HEAD) // (HEAD // 4)
    packed[...] = jnp.broadcast_to(
        jnp.sum(jnp.where(iota(wide.shape, 0) == segment, wide, 0.0), axis=0, keepdims=True),
        packed.shape,
    )
    small[2].wait()
    small[3].wait()
    write_t = write_ref[...].T
    for c in range(pieces):
        part = write_t[:, CHUNK * c : CHUNK * (c + 1)]
        keys[CHUNK * c : CHUNK * (c + 1)] = jnp.concatenate([part, part], axis=1)

    def weigh(turn):
        lanes = pl.ds(pl.multiple_of(turn * LANES, LANES), LANES)
        fetch(turn).wait()
        weight = weight_ref[:, lanes] * 0.5
        state = jnp.zeros((STATE, LANES), F32)
        for c in range(pieces):
            span = slice(CHUNK * c, CHUNK * (c + 1))
            rows = x_ref[span, lanes].astype(F32)
            gain = dot(gains[span], spread[:, lanes])
            sides = []
            for part in range(LANES // 128):
                cols = slice(128 * part, 128 * (part + 1))
                stage[part, 8 + CHUNK * c : 8 + CHUNK * (c + 1)] = rows[:, cols]
                value = conv_silu(stage, part, CHUNK * c, CHUNK, weight[:, cols])
                value_ref[turn, span, cols] = value
                sides.append(jnp.concatenate(split(value * gain[:, cols]), axis=0))
            state = state + dot(keys[span], jnp.concatenate(sides, axis=1))
        leave(turn).start()
        return state

    def finish(turn, state):
        lanes = pl.ds(pl.multiple_of(turn * LANES, LANES), LANES)
        code, scale = encode(state)
        row = iota((EXTRA, LANES), 0)
        first = pltpu.roll(x_ref[0:16, lanes].astype(F32), 7, 0)
        last = pltpu.roll(x_ref[tokens - 16 : tokens, lanes].astype(F32), 7, 0)
        writes = pltpu.roll(write_ref[0:16].astype(F32), 1, 0)
        writes = jnp.concatenate([writes] * (LANES // STATE), axis=1)
        scalar = packed[0:1, lanes]
        high = scalar.astype(BF16).astype(F32)
        middle = (scalar - high).astype(BF16).astype(F32)
        low = scalar - high - middle
        extra = jnp.where(row == 0, scale, 0.0)
        extra = jnp.where((row >= 1) & (row <= 3), writes, extra)
        extra = jnp.where((row >= 4) & (row <= 6), last, extra)
        extra = jnp.where((row >= 7) & (row <= 9), first, extra)
        extra = jnp.where(row == 10, high, extra)
        extra = jnp.where(row == 11, middle, extra)
        extra = jnp.where(row == 12, low, extra).astype(BF16)
        for part in range(LANES // 128):
            place = turn * (LANES // 128) + part
            out_ref[place, 0:STATE] = code[:, 128 * part : 128 * (part + 1)]
            out_ref[place, STATE : STATE + EXTRA] = extra[:, 128 * part : 128 * (part + 1)]

    def pair(i, carry):
        for side in range(2):
            turn = 2 * i + side
            finish(turn, weigh(turn))
            leave_code(turn).start()
        return carry

    lax.fori_loop(0, turns // 2, pair, 0)
    for turn in range(turns):
        leave(turn).wait()
        leave_code(turn).wait()


def in_hbm(*values):
    return [pltpu.with_memory_space_constraint(value, pltpu.HBM) for value in values]


def end_state(x, weight, write, step, decay):
    tokens, channels = x.shape
    heads = step.shape[0]
    owners = channels // 128
    return pl.pallas_call(
        end_state_kernel,
        in_specs=[pl.BlockSpec(memory_space=pltpu.HBM)] * 5,
        out_specs=[pl.BlockSpec(memory_space=pltpu.HBM)] * 2,
        out_shape=[pltpu.HBM((owners, STATE + EXTRA, 128), BF16), pltpu.HBM((tokens, channels), F32)],
        scratch_shapes=[
            pltpu.VMEM(x.shape, BF16),
            pltpu.VMEM(weight.shape, F32),
            pltpu.VMEM(write.shape, BF16),
            pltpu.VMEM(step.shape, F32),
            pltpu.VMEM(decay.shape, F32),
            pltpu.VMEM((tokens, 2 * heads), BF16),
            pltpu.VMEM((2 * heads, channels), BF16),
            pltpu.VMEM((tokens, 2 * CHUNK), BF16),
            pltpu.VMEM((8, channels), F32),
            pltpu.VMEM((LANES // 128, 8 + tokens, 128), F32),
            pltpu.VMEM((owners, STATE + EXTRA, 128), BF16),
            pltpu.VMEM((channels // LANES, tokens, LANES), F32),
            pltpu.SemaphoreType.DMA((3 * (channels // LANES) + 4,)),
        ],
        compiler_params=pltpu.CompilerParams(vmem_limit_bytes=VMEM_BYTES),
        name="end_state",
    )(*in_hbm(x, weight, write, step, decay))


def prefix_kernel(place_ref, in_ref, weight_ref, out_ref, blocks):
    count = in_ref.shape[0]
    tile = in_ref[:, STATE : STATE + EXTRA, :].astype(F32)
    shape = tile.shape
    row, lane = (iota(shape, 1), iota(shape, 2))
    before = jnp.concatenate([jnp.zeros((1,) + shape[1:], F32), tile[:-1]], axis=0)
    rows = jnp.where(
        (row >= 4) & (row <= 6), before, jnp.where((row >= 7) & (row <= 9), tile, 0.0)
    )
    weight = weight_ref[:, pl.ds(pl.multiple_of(place_ref[0] * 128, 128), 128)] * 0.5
    half = rows * weight[3:4][None]
    for back in range(1, TAPS):
        half = half + pltpu.roll(rows, back, 1) * weight[3 - back : 4 - back][None]
    value = silu_of_half(half)
    scalars = jnp.sum(jnp.where((row >= 10) & (row <= 12), tile, 0.0), axis=1, keepdims=True)
    left = iota(scalars.shape, 2) < HEAD

    def spread_of(segment):
        place = segment * (HEAD // 4)
        return jnp.where(
            left, scalars[:, :, place : place + 1], scalars[:, :, HEAD + place : HEAD + place + 1]
        )

    fade = spread_of(0)
    gain = jnp.where(row == 7, spread_of(1), jnp.where(row == 8, spread_of(2), spread_of(3)))
    coarse = value.astype(BF16).astype(F32)
    firsts = jnp.where(row <= 3, pltpu.roll(coarse, EXTRA - 6, 1), pltpu.roll(value - coarse, EXTRA - 3, 1))
    value = jnp.where((row >= 7) & (row <= 9), value * gain, 0.0)
    value = pltpu.roll(value, EXTRA - 6, 1)
    high = value.astype(BF16)
    low = (value - high.astype(F32)).astype(BF16)
    keys = jnp.where((row >= 1) & (row <= 3), tile, 0.0).reshape(count * EXTRA, 128).T.astype(BF16)
    blocks[...] = jnp.zeros(blocks.shape, BF16)
    for j in range(count):
        blocks[EXTRA * j : EXTRA * (j + 1), 128 * j : 128 * (j + 1)] = high[j]
        blocks[EXTRA * (count + j) : EXTRA * (count + j + 1), 128 * j : 128 * (j + 1)] = low[j]
    first = dot(jnp.concatenate([keys, keys], axis=1), blocks[...])
    state = jnp.zeros((STATE, 128), F32)
    top_row = iota((EXTRA, 128), 0) == 0
    for j in range(count):
        state = state + first[:, 128 * j : 128 * (j + 1)]
        code, scale = encode(state)
        out_ref[j, 0:STATE] = code
        out_ref[j, STATE : STATE + EXTRA] = jnp.where(top_row, scale, firsts[j]).astype(BF16)
        local = decode(in_ref[j, 0:STATE], tile[j, 0:1])
        state = fade[j] * state + local


def prefix(place, received, weight):
    count = received.shape[0]
    whole = pl.BlockSpec(memory_space=pltpu.VMEM)
    return pl.pallas_call(
        prefix_kernel,
        in_specs=[pl.BlockSpec(memory_space=pltpu.SMEM), whole, whole],
        out_specs=whole,
        out_shape=jax.ShapeDtypeStruct(received.shape, BF16),
        scratch_shapes=[pltpu.VMEM((2 * count * EXTRA, count * 128), BF16)],
        compiler_params=pltpu.CompilerParams(vmem_limit_bytes=VMEM_BYTES),
        name="prefix",
    )(place, received, weight)


def make_tables(
    write_ref, read_ref, step_ref, decay_ref, skip_ref, gains, fades, reach, keys, mix, rowed
):
    heads, tokens = step_ref.shape
    pieces = tokens // CHUNK
    channels = heads * HEAD
    ones = head_spread(heads, channels)
    logs = stack_chunks(decay_ref[...])
    upto = (iota((CHUNK, CHUNK), 0) <= iota((CHUNK, CHUNK), 1)).astype(F32)
    run = dot_binary(logs, upto)
    middle = run[:, CHUNK // 2 - 1 : CHUNK // 2]
    total = run[:, CHUNK - 1 : CHUNK]
    gain = jnp.exp(middle - run) * stack_chunks(step_ref[...])
    gain = jnp.where((iota(gain.shape, 0) < heads) & (iota(gain.shape, 1) < TAPS - 1), 0.0, gain)
    store_tokens(gains, gain, heads)
    store_tokens(fades, jnp.exp(run - middle), heads)
    lane = iota((heads, 128), 1)
    scalars = jnp.where(lane == pieces, skip_ref[...], 0.0)
    offset = jnp.zeros((heads, 1), F32)
    offsets = []
    for c in range(pieces):
        offsets.append(offset)
        mid = middle[heads * c : heads * (c + 1)]
        tot = total[heads * c : heads * (c + 1)]
        offset = offset + tot
        if c + 1 < pieces:
            onward = jnp.exp(middle[heads * (c + 1) : heads * (c + 2)] + (tot - mid))
            scalars = jnp.where(lane == c, onward, scalars)
    store_tokens(reach, jnp.exp(run + jnp.concatenate(offsets, axis=0)), heads)
    causal = iota((CHUNK, CHUNK), 0) >= iota((CHUNK, CHUNK), 1)
    for c in range(pieces):
        span = slice(CHUNK * c, CHUNK * (c + 1))
        write = write_ref[span]
        read = read_ref[span]
        mixing = lax.dot_general(read, write, (((1,), (1,)), ((), ())), preferred_element_type=F32)
        if c == 0:
            place = pieces + 1
            for t, later in ((0, 1), (0, 2), (1, 2)):
                weight = jnp.exp(run[0:heads, t : t + 1] - run[0:heads, later : later + 1])
                weight = weight * step_ref[:, later : later + 1] * mixing[t : t + 1, later : later + 1]
                scalars = jnp.where(lane == place, weight, scalars)
                place += 1
        high, low = split(jnp.where(causal, mixing, 0.0))
        mix[span] = jnp.concatenate([high, high, low, read, read], axis=1)
        write_t = write.astype(F32).T.astype(BF16)
        keys[span] = jnp.concatenate([write_t, write_t], axis=1)
    rowed[...] = dot_binary(scalars.T[0 : rowed.shape[0]], ones)


def local_slices(
    begin, ready, value_hbm, local_hbm, gains, fades, keys, mix, rowed,
    value_ref, spread, gain0, gain1, fade0, fade1, result, sems,
):
    tokens, width = local_hbm.shape
    pieces = tokens // CHUNK
    channels = rowed.shape[1]
    turns = width // LANES
    wide_gains, wide_fades = (gain0, gain1), (fade0, fade1)

    def columns(turn):
        return pl.ds(pl.multiple_of(turn * LANES, LANES), LANES)

    def fetch(turn):
        return pltpu.make_async_copy(
            value_hbm.at[:, columns(turn + begin)], value_ref.at[turn], sems.at[turn]
        )

    def leave(turn):
        return pltpu.make_async_copy(
            result.at[turn], local_hbm.at[:, columns(turn)], sems.at[turns + turn]
        )

    def widen(turn, side):
        lanes = columns(turn + begin)
        wide_gains[side][...] = dot(gains[...], spread[:, lanes])
        wide_fades[side][...] = dot(fades[...], spread[:, lanes])

    for turn in range(turns):
        fetch(turn).start()
    ones = head_spread(channels // HEAD, channels)
    spread[...] = jnp.concatenate([ones, ones], axis=0).astype(BF16)
    ready()
    widen(0, 0)

    def work(turn, side):
        lanes = columns(turn + begin)
        fetch(turn).wait()
        skip = rowed[pieces : pieces + 1, lanes]
        widen(jnp.minimum(turn + 1, turns - 1), 1 - side)
        state = None
        for c in range(pieces):
            span = slice(CHUNK * c, CHUNK * (c + 1))
            both = jnp.concatenate(split(value_ref[turn, span] * wide_gains[side][span]), axis=0)
            if state is None:
                mixed = dot(mix[span, 0 : 3 * CHUNK], jnp.concatenate([both, both[0:CHUNK]], axis=0))
                state = dot(keys[span], both)
            else:
                high, low = split(state)
                mixed = dot(mix[span], jnp.concatenate([both, both[0:CHUNK], high, low], axis=0))
                if c + 1 < pieces:
                    state = state + dot(keys[span], both)
            if c + 1 < pieces:
                state = state * rowed[c : c + 1, lanes]
            result[turn, span] = mixed * wide_fades[side][span] + skip * value_ref[turn, span]
        leave(turn).start()

    def pair(i, carry):
        for side in range(2):
            work(2 * i + side, side)
        return carry

    lax.fori_loop(0, turns // 2, pair, 0)
    for turn in range(turns):
        leave(turn).wait()


def first_kernel(
    begin, write_hbm, read_hbm, step_hbm, decay_hbm, skip_ref, value_hbm, *refs
):
    outs, local_hbm, ins, tables, rest = refs[0:6], refs[6], refs[7:11], refs[11:17], refs[17:-1]
    sems = refs[-1]
    arrive = [
        pltpu.make_async_copy(source, target, sems.at[i])
        for i, (source, target) in enumerate(
            zip((write_hbm, read_hbm, step_hbm, decay_hbm), ins, strict=True)
        )
    ]
    depart = [
        pltpu.make_async_copy(source, target, sems.at[4 + i])
        for i, (source, target) in enumerate(zip(tables, outs, strict=True))
    ]
    for copy in arrive:
        copy.start()

    def ready():
        for copy in arrive:
            copy.wait()
        make_tables(*ins, skip_ref, *tables)
        for copy in depart:
            copy.start()

    gains, fades, _, keys, mix, rowed = tables
    local_slices(begin, ready, value_hbm, local_hbm, gains, fades, keys, mix, rowed, *rest)
    for copy in depart:
        copy.wait()


def second_kernel(
    begin, gains_hbm, fades_hbm, keys_hbm, mix_hbm, rowed_hbm, value_hbm, local_hbm, *refs
):
    tables, rest, sems = refs[0:5], refs[5:-1], refs[-1]
    arrive = [
        pltpu.make_async_copy(source, target, sems.at[i])
        for i, (source, target) in enumerate(
            zip((gains_hbm, fades_hbm, keys_hbm, mix_hbm, rowed_hbm), tables, strict=True)
        )
    ]
    for copy in arrive:
        copy.start()

    def ready():
        for copy in arrive:
            copy.wait()

    local_slices(begin, ready, value_hbm, local_hbm, *tables, *rest)


def slice_scratch(turns, tokens, channels):
    return [
        pltpu.VMEM((turns, tokens, LANES), F32),
        pltpu.VMEM((2 * (channels // HEAD), channels), BF16),
        pltpu.VMEM((tokens, LANES), F32),
        pltpu.VMEM((tokens, LANES), F32),
        pltpu.VMEM((tokens, LANES), F32),
        pltpu.VMEM((tokens, LANES), F32),
        pltpu.VMEM((turns, tokens, LANES), F32),
        pltpu.SemaphoreType.DMA((2 * turns,)),
    ]


def first_local(turns, write, read, step, decay, skip, value):
    heads, tokens = step.shape
    pieces = tokens // CHUNK
    channels = heads * HEAD
    hbm = pl.BlockSpec(memory_space=pltpu.HBM)
    tables = [
        ((tokens, 2 * heads), BF16),
        ((tokens, 2 * heads), BF16),
        ((tokens, 2 * heads), BF16),
        ((tokens, 2 * CHUNK), BF16),
        ((tokens, 5 * CHUNK), BF16),
        ((pieces + 8, channels), F32),
    ]
    ins = (write, read, step, decay)
    *out, local = pl.pallas_call(
        functools.partial(first_kernel, 0),
        in_specs=[hbm] * 4 + [pl.BlockSpec(memory_space=pltpu.VMEM), hbm],
        out_specs=[hbm] * 7,
        out_shape=[pltpu.HBM(*table) for table in tables]
        + [pltpu.HBM((tokens, turns * LANES), F32)],
        scratch_shapes=[pltpu.VMEM(source.shape, source.dtype) for source in ins]
        + [pltpu.VMEM(*table) for table in tables]
        + slice_scratch(turns, tokens, channels)
        + [pltpu.SemaphoreType.DMA((len(ins) + len(tables),))],
        compiler_params=pltpu.CompilerParams(vmem_limit_bytes=VMEM_BYTES),
        name="first_local",
    )(*in_hbm(*ins), skip, *in_hbm(value))
    return out, local


def second_local(begin, turns, gains, fades, keys, mix, rowed, value):
    tokens, channels = value.shape
    hbm = pl.BlockSpec(memory_space=pltpu.HBM)
    tables = (gains, fades, keys, mix, rowed)
    return pl.pallas_call(
        functools.partial(second_kernel, begin),
        in_specs=[hbm] * 6,
        out_specs=hbm,
        out_shape=pltpu.HBM((tokens, turns * LANES), F32),
        scratch_shapes=[pltpu.VMEM(table.shape, table.dtype) for table in tables]
        + slice_scratch(turns, tokens, channels)
        + [pltpu.SemaphoreType.DMA((len(tables),))],
        compiler_params=pltpu.CompilerParams(vmem_limit_bytes=VMEM_BYTES),
        name="second_local",
    )(*in_hbm(*tables, value))


def final_kernel(
    state_ref, gain_ref, read_hbm, fade_hbm, rowed_hbm, left_hbm, right_hbm, gate_hbm, out_hbm,
    read_ref, fade_ref, rowed, local_ref, gate_ref, states, spread, gated, out_ref, sems,
):
    owners = state_ref.shape[0]
    channels = owners * 128
    tokens = read_ref.shape[0]
    heads = channels // HEAD
    turns = tokens // CHUNK

    def rows(turn):
        return pl.ds(pl.multiple_of(turn * CHUNK, CHUNK), CHUNK)

    def fetch(turn):
        half = left_hbm.shape[1]
        moves = (
            (left_hbm.at[rows(turn)], local_ref.at[rows(turn), 0:half]),
            (right_hbm.at[rows(turn)], local_ref.at[rows(turn), half:channels]),
            (gate_hbm.at[rows(turn)], gate_ref.at[rows(turn)]),
        )
        return [
            pltpu.make_async_copy(source, target, sems.at[i, turn])
            for i, (source, target) in enumerate(moves)
        ]

    def leave(turn):
        return pltpu.make_async_copy(out_ref.at[rows(turn)], out_hbm.at[rows(turn)], sems.at[4, turn])

    small = [
        pltpu.make_async_copy(read_hbm, read_ref, sems.at[3, 2]),
        pltpu.make_async_copy(fade_hbm, fade_ref, sems.at[3, 3]),
        pltpu.make_async_copy(rowed_hbm, rowed, sems.at[3, 4]),
    ]
    for copy in small:
        copy.start()
    for turn in range(turns):
        for copy in fetch(turn):
            copy.start()
    ones = head_spread(heads, channels)
    spread[...] = jnp.concatenate([ones, ones], axis=0).astype(BF16)
    for k in range(owners):
        value = decode(state_ref[k, 0:STATE], state_ref[k, STATE : STATE + 1].astype(F32))
        high, low = split(value)
        states[0:STATE, 128 * k : 128 * (k + 1)] = high
        states[STATE : 2 * STATE, 128 * k : 128 * (k + 1)] = low
    for copy in small:
        copy.wait()
    for copy in fetch(0):
        copy.wait()
    pieces = tokens // CHUNK
    row = iota((8, 128), 0)
    for k in range(owners):
        lanes = slice(128 * k, 128 * (k + 1))
        firsts = state_ref[k, STATE : STATE + EXTRA].astype(F32)
        value0, value1, value2 = (firsts[t : t + 1] + firsts[t + 3 : t + 4] for t in (1, 2, 3))
        skip, mix01, mix02, mix12 = (rowed[pieces + i : pieces + i + 1, lanes] for i in range(4))
        patch = jnp.where(row == 2, skip * value2, local_ref[0:8, lanes])
        patch = jnp.where(row == 1, skip * value1 - mix12 * value2, patch)
        patch = jnp.where(row == 0, skip * value0 - mix01 * value1 - mix02 * value2, patch)
        local_ref[0:8, lanes] = patch

    def work(turn):
        span = rows(turn)
        read = read_ref[span]
        both = jnp.concatenate([read, read], axis=1)
        fade = fade_ref[span]
        squares = jnp.zeros((CHUNK, 128), F32)
        for j in range(channels // LANES):
            lanes = slice(LANES * j, LANES * (j + 1))
            reach = dot(both, states[:, lanes]) * dot(fade, spread[:, lanes])
            opened = silu_of_half((gate_ref[span, lanes] * 0.5).astype(F32))
            part = (local_ref[span, lanes] + reach) * opened
            gated[:, lanes] = part
            for i in range(LANES // 128):
                piece = part[:, 128 * i : 128 * (i + 1)]
                squares = squares + piece * piece
        inverse = lax.rsqrt(jnp.sum(squares, axis=1, keepdims=True) * (1.0 / channels) + 1e-05)
        for j in range(channels // LANES):
            lanes = slice(LANES * j, LANES * (j + 1))
            out_ref[span, lanes] = (gated[:, lanes] * inverse * gain_ref[:, lanes]).astype(BF16)
        leave(turn).start()

    work(0)

    def later(turn, carry):
        for copy in fetch(turn):
            copy.wait()
        work(turn)
        return carry

    lax.fori_loop(1, turns, later, 0)
    for turn in range(turns):
        leave(turn).wait()


def final_part(entering, norm_gain, read, fade, rowed, left, right, gate):
    tokens, channels = gate.shape
    heads = channels // HEAD
    hbm = pl.BlockSpec(memory_space=pltpu.HBM)
    vmem = pl.BlockSpec(memory_space=pltpu.VMEM)
    return pl.pallas_call(
        final_kernel,
        in_specs=[vmem] * 2 + [hbm] * 6,
        out_specs=hbm,
        out_shape=pltpu.HBM((tokens, channels), BF16),
        scratch_shapes=[
            pltpu.VMEM(read.shape, BF16),
            pltpu.VMEM(fade.shape, BF16),
            pltpu.VMEM(rowed.shape, F32),
            pltpu.VMEM((tokens, channels), F32),
            pltpu.VMEM(gate.shape, BF16),
            pltpu.VMEM((2 * STATE, channels), BF16),
            pltpu.VMEM((2 * heads, channels), BF16),
            pltpu.VMEM((CHUNK, channels), F32),
            pltpu.VMEM((tokens, channels), BF16),
            pltpu.SemaphoreType.DMA((5, tokens // CHUNK)),
        ],
        compiler_params=pltpu.CompilerParams(vmem_limit_bytes=VMEM_BYTES),
        name="final_part",
    )(entering, norm_gain, *in_hbm(read, fade, rowed, left, right, gate))


def shards(x, weight, gate, write, read, step, decay, skip, norm_gain):
    place = lax.axis_index("ctx")
    turns = x.shape[1] // LANES
    ends, value = end_state(x, weight, write, step, decay)
    received = lax.all_to_all(ends, "ctx", 0, 0)
    decay, ends = lax.optimization_barrier((decay, ends))
    part = turns // 2
    tables, left = first_local(part, write, read, step, decay, skip[:, None], value)
    gains, fades, reach, keys, mix, rowed = tables
    received, left = lax.optimization_barrier((received, left))
    entering = prefix(place[None], received, weight)
    value, entering = lax.optimization_barrier((value, entering))
    entering = lax.all_to_all(entering, "ctx", 0, 0)
    right = second_local(part, turns - part, gains, fades, keys, mix, rowed, value)
    return final_part(entering, norm_gain[None, :], read, reach, rowed, left, right, gate)


def solution(mesh):
    placed = (
        P("ctx", "tp"),
        P(None, "tp"),
        P("ctx", "tp"),
        P("ctx", "tp"),
        P("ctx", "tp"),
        P("tp", "ctx"),
        P("tp", "ctx"),
        P("tp"),
        P("tp"),
    )
    return jax.shard_map(
        shards, mesh=mesh, in_specs=placed, out_specs=P("ctx", "tp"), check_vma=False
    )
```

```python
import functools

import jax
import jax.numpy as jnp
from jax import lax
from jax.experimental import pallas as pl
from jax.experimental.pallas import tpu as pltpu
from jax.sharding import PartitionSpec as P

F32 = jnp.float32
BF16 = jnp.bfloat16
HEAD = 64
STATE = 128
TAPS = 4
CHUNK = 128
LANES = 256
EXTRA = 16
VMEM_BYTES = 24 * 1024 * 1024


def iota(shape, dim):
    return lax.broadcasted_iota(jnp.int32, shape, dim)


def dot(a, b):
    return jnp.dot(a, b, preferred_element_type=F32)


def dot_binary(a, b):
    high = a.astype(BF16)
    rest = a - high.astype(F32)
    middle = rest.astype(BF16)
    low = (rest - middle.astype(F32)).astype(BF16)
    b = b.astype(BF16)
    return dot(jnp.concatenate([high, middle, low], axis=1), jnp.concatenate([b, b, b], axis=0))


def split(value):
    high = value.astype(BF16)
    return high, (value - high.astype(F32)).astype(BF16)


def silu_of_half(half):
    return half * jnp.tanh(half) + half


def encode(value):
    top = jnp.max(jnp.abs(value), axis=0, keepdims=True)
    scale = jnp.maximum(top * 1.00390625, 1e-30).astype(BF16).astype(F32)
    return jnp.exp2(value * (126.0 / scale)).astype(BF16), scale


def decode(code, scale):
    return jnp.log2(code.astype(F32)) * (scale * (1.0 / 126.0))


def stack_chunks(value):
    pieces = value.shape[1] // CHUNK
    return jnp.concatenate([value[:, CHUNK * c : CHUNK * (c + 1)] for c in range(pieces)], axis=0)


def head_spread(heads, channels):
    return (iota((heads, channels), 0) == iota((heads, channels), 1) // HEAD).astype(F32)


def store_tokens(ref, value, heads):
    for c in range(value.shape[0] // heads):
        part = value[heads * c : heads * (c + 1)]
        high = part.astype(BF16).astype(F32)
        both = jnp.concatenate([high, part - high], axis=0)
        ref[CHUNK * c : CHUNK * (c + 1), :] = both.T.astype(BF16)


def conv_half(rows, weight):
    weight = weight * 0.5
    back = pltpu.roll(rows, 1, 0)
    near = rows * weight[3:4] + back * weight[2:3]
    far = rows * weight[1:2] + back * weight[0:1]
    return (near + pltpu.roll(far, 2, 0))[16:]


def conv_silu(stage, part, start, count, weight):
    half = stage[part, pl.ds(start + 8, count)] * weight[3:4]
    for back in range(1, TAPS):
        half = half + stage[part, pl.ds(start + 8 - back, count)] * weight[3 - back : 4 - back]
    return silu_of_half(half)


def end_state_kernel(
    x_hbm, weight_hbm, write_hbm, step_hbm, decay_hbm, out_hbm, value_hbm,
    x_ref, weight_ref, write_ref, step_ref, decay_ref, gains, spread, keys, packed, stage, out_ref, value_ref, sems,
):
    heads, tokens = step_ref.shape
    pieces = tokens // CHUNK
    channels = heads * HEAD
    turns = channels // LANES
    small = [
        pltpu.make_async_copy(source, target, sems.at[turns + i])
        for i, (source, target) in enumerate(
            ((decay_hbm, decay_ref), (step_hbm, step_ref), (write_hbm, write_ref), (weight_hbm, weight_ref))
        )
    ]

    def fetch(turn):
        lanes = pl.ds(pl.multiple_of(turn * LANES, LANES), LANES)
        return pltpu.make_async_copy(x_hbm.at[:, lanes], x_ref.at[:, lanes], sems.at[turn])

    def leave(turn):
        lanes = pl.ds(pl.multiple_of(turn * LANES, LANES), LANES)
        return pltpu.make_async_copy(
            value_ref.at[turn], value_hbm.at[:, lanes], sems.at[2 * turns + 4 + turn]
        )

    def leave_code(turn):
        places = pl.ds(turn * (LANES // 128), LANES // 128)
        return pltpu.make_async_copy(out_ref.at[places], out_hbm.at[places], sems.at[turns + 4 + turn])

    for copy in small:
        copy.start()
    for turn in range(turns):
        fetch(turn).start()
    ones = head_spread(heads, channels)
    spread[...] = jnp.concatenate([ones, ones], axis=0).astype(BF16)
    for part in range(LANES // 128):
        stage[part, 0:8] = jnp.zeros((8, 128), F32)
    small[0].wait()
    small[1].wait()
    decay = decay_ref[...]
    logs = stack_chunks(decay)
    later = (iota((CHUNK, CHUNK), 0) > iota((CHUNK, CHUNK), 1)).astype(F32)
    suffix = dot_binary(logs, later)
    total = suffix[:, 0:1] + logs[:, 0:1]
    offset = jnp.zeros((heads, 1), F32)
    offsets = []
    for c in reversed(range(pieces)):
        offsets.append(offset)
        offset = offset + total[heads * c : heads * (c + 1)]
    suffix = suffix + jnp.concatenate(offsets[::-1], axis=0)
    gain = jnp.exp(suffix) * stack_chunks(step_ref[...])
    row, lane = (iota(gain.shape, 0), iota(gain.shape, 1))
    gain = jnp.where((row < heads) & (lane < TAPS - 1), 0.0, gain)
    store_tokens(gains, gain, heads)
    first = decay[:, 0:CHUNK]
    lane = iota(first.shape, 1)
    run0 = first[:, 0:1]
    run1 = run0 + first[:, 1:2]
    run2 = run1 + first[:, 2:3]
    step = step_ref[:, 0:CHUNK]
    scalars = jnp.where(lane == 0, jnp.exp(offset), 0.0)
    for t, run in enumerate((run0, run1, run2)):
        scalars = jnp.where(lane == t + 1, jnp.exp(-run) * step[:, t : t + 1], scalars)
    wide = dot_binary(scalars.T[0:8], ones)
    segment = (iota(wide.shape, 1) % HEAD) // (HEAD // 4)
    packed[...] = jnp.broadcast_to(
        jnp.sum(jnp.where(iota(wide.shape, 0) == segment, wide, 0.0), axis=0, keepdims=True),
        packed.shape,
    )
    small[2].wait()
    small[3].wait()
    write_t = write_ref[...].T
    for c in range(pieces):
        part = write_t[:, CHUNK * c : CHUNK * (c + 1)]
        keys[CHUNK * c : CHUNK * (c + 1)] = jnp.concatenate([part, part], axis=1)

    def weigh(turn):
        lanes = pl.ds(pl.multiple_of(turn * LANES, LANES), LANES)
        fetch(turn).wait()
        weight = weight_ref[:, lanes] * 0.5
        state = jnp.zeros((STATE, LANES), F32)
        held = []
        for c in range(pieces):
            span = slice(CHUNK * c, CHUNK * (c + 1))
            rows = x_ref[span, lanes].astype(F32)
            gain = dot(gains[span], spread[:, lanes])
            sides = []
            for part in range(LANES // 128):
                cols = slice(128 * part, 128 * (part + 1))
                stage[part, 8 + CHUNK * c : 8 + CHUNK * (c + 1)] = rows[:, cols]
                value = conv_silu(stage, part, CHUNK * c, CHUNK, weight[:, cols])
                value_ref[turn, span, cols] = value
                sides.append(jnp.concatenate(split(value * gain[:, cols]), axis=0))
            held.append((keys[span], jnp.concatenate(sides, axis=1)))
            if len(held) == 2:
                left, right = zip(*held, strict=True)
                part = dot(jnp.concatenate(left, axis=1), jnp.concatenate(right, axis=0))
                state = part if c < 2 else state + part
                held = []
        leave(turn).start()
        return state

    def finish(turn, state):
        lanes = pl.ds(pl.multiple_of(turn * LANES, LANES), LANES)
        code, scale = encode(state)
        row = iota((EXTRA, LANES), 0)
        first = pltpu.roll(x_ref[0:16, lanes].astype(F32), 7, 0)
        last = pltpu.roll(x_ref[tokens - 16 : tokens, lanes].astype(F32), 7, 0)
        writes = pltpu.roll(write_ref[0:16].astype(F32), 1, 0)
        writes = jnp.concatenate([writes] * (LANES // STATE), axis=1)
        scalar = packed[0:1, lanes]
        high = scalar.astype(BF16).astype(F32)
        middle = (scalar - high).astype(BF16).astype(F32)
        low = scalar - high - middle
        extra = jnp.where(row == 0, scale, 0.0)
        extra = jnp.where((row >= 1) & (row <= 3), writes, extra)
        extra = jnp.where((row >= 4) & (row <= 6), last, extra)
        extra = jnp.where((row >= 7) & (row <= 9), first, extra)
        extra = jnp.where(row == 10, high, extra)
        extra = jnp.where(row == 11, middle, extra)
        extra = jnp.where(row == 12, low, extra).astype(BF16)
        for part in range(LANES // 128):
            place = turn * (LANES // 128) + part
            out_ref[place, 0:STATE] = code[:, 128 * part : 128 * (part + 1)]
            out_ref[place, STATE : STATE + EXTRA] = extra[:, 128 * part : 128 * (part + 1)]

    def pair(i, carry):
        for side in range(2):
            turn = 2 * i + side
            finish(turn, weigh(turn))
            leave_code(turn).start()
        return carry

    lax.fori_loop(0, turns // 2, pair, 0)
    for turn in range(turns):
        leave(turn).wait()
        leave_code(turn).wait()


def in_hbm(*values):
    return [pltpu.with_memory_space_constraint(value, pltpu.HBM) for value in values]


def end_state(x, weight, write, step, decay):
    tokens, channels = x.shape
    heads = step.shape[0]
    owners = channels // 128
    return pl.pallas_call(
        end_state_kernel,
        in_specs=[pl.BlockSpec(memory_space=pltpu.HBM)] * 5,
        out_specs=[pl.BlockSpec(memory_space=pltpu.HBM)] * 2,
        out_shape=[pltpu.HBM((owners, STATE + EXTRA, 128), BF16), pltpu.HBM((tokens, channels), F32)],
        scratch_shapes=[
            pltpu.VMEM(x.shape, BF16),
            pltpu.VMEM(weight.shape, F32),
            pltpu.VMEM(write.shape, BF16),
            pltpu.VMEM(step.shape, F32),
            pltpu.VMEM(decay.shape, F32),
            pltpu.VMEM((tokens, 2 * heads), BF16),
            pltpu.VMEM((2 * heads, channels), BF16),
            pltpu.VMEM((tokens, 2 * CHUNK), BF16),
            pltpu.VMEM((8, channels), F32),
            pltpu.VMEM((LANES // 128, 8 + tokens, 128), F32),
            pltpu.VMEM((owners, STATE + EXTRA, 128), BF16),
            pltpu.VMEM((channels // LANES, tokens, LANES), F32),
            pltpu.SemaphoreType.DMA((3 * (channels // LANES) + 4,)),
        ],
        compiler_params=pltpu.CompilerParams(vmem_limit_bytes=VMEM_BYTES),
        name="end_state",
    )(*in_hbm(x, weight, write, step, decay))


def prefix_kernel(place_ref, in_ref, weight_ref, out_ref, blocks):
    count = in_ref.shape[0]
    tile = in_ref[:, STATE : STATE + EXTRA, :].astype(F32)
    shape = tile.shape
    row, lane = (iota(shape, 1), iota(shape, 2))
    before = jnp.concatenate([jnp.zeros((1,) + shape[1:], F32), tile[:-1]], axis=0)
    rows = jnp.where(
        (row >= 4) & (row <= 6), before, jnp.where((row >= 7) & (row <= 9), tile, 0.0)
    )
    weight = weight_ref[:, pl.ds(pl.multiple_of(place_ref[0] * 128, 128), 128)] * 0.5
    half = rows * weight[3:4][None]
    for back in range(1, TAPS):
        half = half + pltpu.roll(rows, back, 1) * weight[3 - back : 4 - back][None]
    value = silu_of_half(half)
    scalars = jnp.sum(jnp.where((row >= 10) & (row <= 12), tile, 0.0), axis=1, keepdims=True)
    left = iota(scalars.shape, 2) < HEAD

    def spread_of(segment):
        place = segment * (HEAD // 4)
        return jnp.where(
            left, scalars[:, :, place : place + 1], scalars[:, :, HEAD + place : HEAD + place + 1]
        )

    fade = spread_of(0)
    gain = jnp.where(row == 7, spread_of(1), jnp.where(row == 8, spread_of(2), spread_of(3)))
    coarse = value.astype(BF16).astype(F32)
    firsts = jnp.where(row <= 3, pltpu.roll(coarse, EXTRA - 6, 1), pltpu.roll(value - coarse, EXTRA - 3, 1))
    value = jnp.where((row >= 7) & (row <= 9), value * gain, 0.0)
    value = pltpu.roll(value, EXTRA - 6, 1)
    high = value.astype(BF16)
    low = (value - high.astype(F32)).astype(BF16)
    keys = jnp.where((row >= 1) & (row <= 3), tile, 0.0).reshape(count * EXTRA, 128).T.astype(BF16)
    blocks[...] = jnp.zeros(blocks.shape, BF16)
    for j in range(count):
        blocks[EXTRA * j : EXTRA * (j + 1), 128 * j : 128 * (j + 1)] = high[j]
        blocks[EXTRA * (count + j) : EXTRA * (count + j + 1), 128 * j : 128 * (j + 1)] = low[j]
    first = dot(jnp.concatenate([keys, keys], axis=1), blocks[...])
    state = jnp.zeros((STATE, 128), F32)
    top_row = iota((EXTRA, 128), 0) == 0
    for j in range(count):
        state = state + first[:, 128 * j : 128 * (j + 1)]
        code, scale = encode(state)
        out_ref[j, 0:STATE] = code
        out_ref[j, STATE : STATE + EXTRA] = jnp.where(top_row, scale, firsts[j]).astype(BF16)
        local = decode(in_ref[j, 0:STATE], tile[j, 0:1])
        state = fade[j] * state + local


def prefix(place, received, weight):
    count = received.shape[0]
    whole = pl.BlockSpec(memory_space=pltpu.VMEM)
    return pl.pallas_call(
        prefix_kernel,
        in_specs=[pl.BlockSpec(memory_space=pltpu.SMEM), whole, whole],
        out_specs=whole,
        out_shape=jax.ShapeDtypeStruct(received.shape, BF16),
        scratch_shapes=[pltpu.VMEM((2 * count * EXTRA, count * 128), BF16)],
        compiler_params=pltpu.CompilerParams(vmem_limit_bytes=VMEM_BYTES),
        name="prefix",
    )(place, received, weight)


def make_tables(
    write_ref, read_ref, step_ref, decay_ref, skip_ref, gains, fades, reach, keys, mix, rowed
):
    heads, tokens = step_ref.shape
    pieces = tokens // CHUNK
    channels = heads * HEAD
    ones = head_spread(heads, channels)
    logs = stack_chunks(decay_ref[...])
    upto = (iota((CHUNK, CHUNK), 0) <= iota((CHUNK, CHUNK), 1)).astype(F32)
    run = dot_binary(logs, upto)
    middle = run[:, CHUNK // 2 - 1 : CHUNK // 2]
    total = run[:, CHUNK - 1 : CHUNK]
    gain = jnp.exp(middle - run) * stack_chunks(step_ref[...])
    gain = jnp.where((iota(gain.shape, 0) < heads) & (iota(gain.shape, 1) < TAPS - 1), 0.0, gain)
    store_tokens(gains, gain, heads)
    store_tokens(fades, jnp.exp(run - middle), heads)
    lane = iota((heads, 128), 1)
    scalars = jnp.where(lane == pieces, skip_ref[...], 0.0)
    offset = jnp.zeros((heads, 1), F32)
    offsets = []
    for c in range(pieces):
        offsets.append(offset)
        mid = middle[heads * c : heads * (c + 1)]
        tot = total[heads * c : heads * (c + 1)]
        offset = offset + tot
        if c + 1 < pieces:
            onward = jnp.exp(middle[heads * (c + 1) : heads * (c + 2)] + (tot - mid))
            scalars = jnp.where(lane == c, onward, scalars)
    store_tokens(reach, jnp.exp(run + jnp.concatenate(offsets, axis=0)), heads)
    causal = iota((CHUNK, CHUNK), 0) >= iota((CHUNK, CHUNK), 1)
    for c in range(pieces):
        span = slice(CHUNK * c, CHUNK * (c + 1))
        write = write_ref[span]
        read = read_ref[span]
        mixing = lax.dot_general(read, write, (((1,), (1,)), ((), ())), preferred_element_type=F32)
        if c == 0:
            place = pieces + 1
            for t, later in ((0, 1), (0, 2), (1, 2)):
                weight = jnp.exp(run[0:heads, t : t + 1] - run[0:heads, later : later + 1])
                weight = weight * step_ref[:, later : later + 1] * mixing[t : t + 1, later : later + 1]
                scalars = jnp.where(lane == place, weight, scalars)
                place += 1
        high, low = split(jnp.where(causal, mixing, 0.0))
        mix[span] = jnp.concatenate([high, high, low, read, read], axis=1)
        write_t = write.astype(F32).T.astype(BF16)
        keys[span] = jnp.concatenate([write_t, write_t], axis=1)
    rowed[...] = dot_binary(scalars.T[0 : rowed.shape[0]], ones)


def local_slices(
    begin, ready, value_hbm, local_hbm, gains, fades, keys, mix, rowed,
    value_ref, spread, gain0, gain1, fade0, fade1, result, sems,
):
    tokens, width = local_hbm.shape
    pieces = tokens // CHUNK
    channels = rowed.shape[1]
    turns = width // LANES
    wide_gains, wide_fades = (gain0, gain1), (fade0, fade1)

    def columns(turn):
        return pl.ds(pl.multiple_of(turn * LANES, LANES), LANES)

    def fetch(turn):
        return pltpu.make_async_copy(
            value_hbm.at[:, columns(turn + begin)], value_ref.at[turn], sems.at[turn]
        )

    def leave(turn):
        return pltpu.make_async_copy(
            result.at[turn], local_hbm.at[:, columns(turn)], sems.at[turns + turn]
        )

    def widen(turn, side):
        lanes = columns(turn + begin)
        wide_gains[side][...] = dot(gains[...], spread[:, lanes])
        wide_fades[side][...] = dot(fades[...], spread[:, lanes])

    for turn in range(turns):
        fetch(turn).start()
    ones = head_spread(channels // HEAD, channels)
    spread[...] = jnp.concatenate([ones, ones], axis=0).astype(BF16)
    ready()
    widen(0, 0)

    def work(turn, side):
        lanes = columns(turn + begin)
        fetch(turn).wait()
        skip = rowed[pieces : pieces + 1, lanes]
        widen(jnp.minimum(turn + 1, turns - 1), 1 - side)
        state = None
        for c in range(pieces):
            span = slice(CHUNK * c, CHUNK * (c + 1))
            both = jnp.concatenate(split(value_ref[turn, span] * wide_gains[side][span]), axis=0)
            if state is None:
                mixed = dot(mix[span, 0 : 3 * CHUNK], jnp.concatenate([both, both[0:CHUNK]], axis=0))
                state = dot(keys[span], both)
            else:
                high, low = split(state)
                mixed = dot(mix[span], jnp.concatenate([both, both[0:CHUNK], high, low], axis=0))
                if c + 1 < pieces:
                    state = state + dot(keys[span], both)
            if c + 1 < pieces:
                state = state * rowed[c : c + 1, lanes]
            result[turn, span] = mixed * wide_fades[side][span] + skip * value_ref[turn, span]
        leave(turn).start()

    def pair(i, carry):
        for side in range(2):
            work(2 * i + side, side)
        return carry

    lax.fori_loop(0, turns // 2, pair, 0)
    for turn in range(turns):
        leave(turn).wait()


def first_kernel(
    begin, write_hbm, read_hbm, step_hbm, decay_hbm, skip_ref, value_hbm, *refs
):
    outs, local_hbm, ins, tables, rest = refs[0:6], refs[6], refs[7:11], refs[11:17], refs[17:-1]
    sems = refs[-1]
    arrive = [
        pltpu.make_async_copy(source, target, sems.at[i])
        for i, (source, target) in enumerate(
            zip((write_hbm, read_hbm, step_hbm, decay_hbm), ins, strict=True)
        )
    ]
    depart = [
        pltpu.make_async_copy(source, target, sems.at[4 + i])
        for i, (source, target) in enumerate(zip(tables, outs, strict=True))
    ]
    for copy in arrive:
        copy.start()

    def ready():
        for copy in arrive:
            copy.wait()
        make_tables(*ins, skip_ref, *tables)
        for copy in depart:
            copy.start()

    gains, fades, _, keys, mix, rowed = tables
    local_slices(begin, ready, value_hbm, local_hbm, gains, fades, keys, mix, rowed, *rest)
    for copy in depart:
        copy.wait()


def second_kernel(
    begin, gains_hbm, fades_hbm, keys_hbm, mix_hbm, rowed_hbm, value_hbm, local_hbm, *refs
):
    tables, rest, sems = refs[0:5], refs[5:-1], refs[-1]
    arrive = [
        pltpu.make_async_copy(source, target, sems.at[i])
        for i, (source, target) in enumerate(
            zip((gains_hbm, fades_hbm, keys_hbm, mix_hbm, rowed_hbm), tables, strict=True)
        )
    ]
    for copy in arrive:
        copy.start()

    def ready():
        for copy in arrive:
            copy.wait()

    local_slices(begin, ready, value_hbm, local_hbm, *tables, *rest)


def slice_scratch(turns, tokens, channels):
    return [
        pltpu.VMEM((turns, tokens, LANES), F32),
        pltpu.VMEM((2 * (channels // HEAD), channels), BF16),
        pltpu.VMEM((tokens, LANES), F32),
        pltpu.VMEM((tokens, LANES), F32),
        pltpu.VMEM((tokens, LANES), F32),
        pltpu.VMEM((tokens, LANES), F32),
        pltpu.VMEM((turns, tokens, LANES), F32),
        pltpu.SemaphoreType.DMA((2 * turns,)),
    ]


def first_local(turns, write, read, step, decay, skip, value):
    heads, tokens = step.shape
    pieces = tokens // CHUNK
    channels = heads * HEAD
    hbm = pl.BlockSpec(memory_space=pltpu.HBM)
    tables = [
        ((tokens, 2 * heads), BF16),
        ((tokens, 2 * heads), BF16),
        ((tokens, 2 * heads), BF16),
        ((tokens, 2 * CHUNK), BF16),
        ((tokens, 5 * CHUNK), BF16),
        ((pieces + 8, channels), F32),
    ]
    ins = (write, read, step, decay)
    *out, local = pl.pallas_call(
        functools.partial(first_kernel, 0),
        in_specs=[hbm] * 4 + [pl.BlockSpec(memory_space=pltpu.VMEM), hbm],
        out_specs=[hbm] * 7,
        out_shape=[pltpu.HBM(*table) for table in tables]
        + [pltpu.HBM((tokens, turns * LANES), F32)],
        scratch_shapes=[pltpu.VMEM(source.shape, source.dtype) for source in ins]
        + [pltpu.VMEM(*table) for table in tables]
        + slice_scratch(turns, tokens, channels)
        + [pltpu.SemaphoreType.DMA((len(ins) + len(tables),))],
        compiler_params=pltpu.CompilerParams(vmem_limit_bytes=VMEM_BYTES),
        name="first_local",
    )(*in_hbm(*ins), skip, *in_hbm(value))
    return out, local


def second_local(begin, turns, gains, fades, keys, mix, rowed, value):
    tokens, channels = value.shape
    hbm = pl.BlockSpec(memory_space=pltpu.HBM)
    tables = (gains, fades, keys, mix, rowed)
    return pl.pallas_call(
        functools.partial(second_kernel, begin),
        in_specs=[hbm] * 6,
        out_specs=hbm,
        out_shape=pltpu.HBM((tokens, turns * LANES), F32),
        scratch_shapes=[pltpu.VMEM(table.shape, table.dtype) for table in tables]
        + slice_scratch(turns, tokens, channels)
        + [pltpu.SemaphoreType.DMA((len(tables),))],
        compiler_params=pltpu.CompilerParams(vmem_limit_bytes=VMEM_BYTES),
        name="second_local",
    )(*in_hbm(*tables, value))


def final_kernel(
    state_ref, gain_ref, read_hbm, fade_hbm, rowed_hbm, left_hbm, right_hbm, gate_hbm, out_hbm,
    read_ref, fade_ref, rowed, local_ref, gate_ref, states, spread, gated, out_ref, sems,
):
    owners = state_ref.shape[0]
    channels = owners * 128
    tokens = read_ref.shape[0]
    heads = channels // HEAD
    turns = tokens // CHUNK

    def rows(turn):
        return pl.ds(pl.multiple_of(turn * CHUNK, CHUNK), CHUNK)

    def fetch(turn):
        half = left_hbm.shape[1]
        moves = (
            (left_hbm.at[rows(turn)], local_ref.at[rows(turn), 0:half]),
            (right_hbm.at[rows(turn)], local_ref.at[rows(turn), half:channels]),
            (gate_hbm.at[rows(turn)], gate_ref.at[rows(turn)]),
        )
        return [
            pltpu.make_async_copy(source, target, sems.at[i, turn])
            for i, (source, target) in enumerate(moves)
        ]

    def leave(turn):
        return pltpu.make_async_copy(out_ref.at[rows(turn)], out_hbm.at[rows(turn)], sems.at[4, turn])

    small = [
        pltpu.make_async_copy(read_hbm, read_ref, sems.at[3, 2]),
        pltpu.make_async_copy(fade_hbm, fade_ref, sems.at[3, 3]),
        pltpu.make_async_copy(rowed_hbm, rowed, sems.at[3, 4]),
    ]
    for copy in small:
        copy.start()
    for turn in range(turns):
        for copy in fetch(turn):
            copy.start()
    ones = head_spread(heads, channels)
    spread[...] = jnp.concatenate([ones, ones], axis=0).astype(BF16)
    for k in range(owners):
        value = decode(state_ref[k, 0:STATE], state_ref[k, STATE : STATE + 1].astype(F32))
        high, low = split(value)
        states[0:STATE, 128 * k : 128 * (k + 1)] = high
        states[STATE : 2 * STATE, 128 * k : 128 * (k + 1)] = low
    for copy in small:
        copy.wait()
    for copy in fetch(0):
        copy.wait()
    pieces = tokens // CHUNK
    row = iota((8, 128), 0)
    for k in range(owners):
        lanes = slice(128 * k, 128 * (k + 1))
        firsts = state_ref[k, STATE : STATE + EXTRA].astype(F32)
        value0, value1, value2 = (firsts[t : t + 1] + firsts[t + 3 : t + 4] for t in (1, 2, 3))
        skip, mix01, mix02, mix12 = (rowed[pieces + i : pieces + i + 1, lanes] for i in range(4))
        patch = jnp.where(row == 2, skip * value2, local_ref[0:8, lanes])
        patch = jnp.where(row == 1, skip * value1 - mix12 * value2, patch)
        patch = jnp.where(row == 0, skip * value0 - mix01 * value1 - mix02 * value2, patch)
        local_ref[0:8, lanes] = patch

    def work(turn):
        span = rows(turn)
        read = read_ref[span]
        both = jnp.concatenate([read, read], axis=1)
        fade = fade_ref[span]
        squares = jnp.zeros((CHUNK, 128), F32)
        for j in range(channels // LANES):
            lanes = slice(LANES * j, LANES * (j + 1))
            reach = dot(both, states[:, lanes]) * dot(fade, spread[:, lanes])
            opened = silu_of_half((gate_ref[span, lanes] * 0.5).astype(F32))
            part = (local_ref[span, lanes] + reach) * opened
            gated[:, lanes] = part
            for i in range(LANES // 128):
                piece = part[:, 128 * i : 128 * (i + 1)]
                squares = squares + piece * piece
        inverse = lax.rsqrt(jnp.sum(squares, axis=1, keepdims=True) * (1.0 / channels) + 1e-05)
        for j in range(channels // LANES):
            lanes = slice(LANES * j, LANES * (j + 1))
            out_ref[span, lanes] = (gated[:, lanes] * inverse * gain_ref[:, lanes]).astype(BF16)
        leave(turn).start()

    work(0)

    def later(turn, carry):
        for copy in fetch(turn):
            copy.wait()
        work(turn)
        return carry

    lax.fori_loop(1, turns, later, 0)
    for turn in range(turns):
        leave(turn).wait()


def final_part(entering, norm_gain, read, fade, rowed, left, right, gate):
    tokens, channels = gate.shape
    heads = channels // HEAD
    hbm = pl.BlockSpec(memory_space=pltpu.HBM)
    vmem = pl.BlockSpec(memory_space=pltpu.VMEM)
    return pl.pallas_call(
        final_kernel,
        in_specs=[vmem] * 2 + [hbm] * 6,
        out_specs=hbm,
        out_shape=pltpu.HBM((tokens, channels), BF16),
        scratch_shapes=[
            pltpu.VMEM(read.shape, BF16),
            pltpu.VMEM(fade.shape, BF16),
            pltpu.VMEM(rowed.shape, F32),
            pltpu.VMEM((tokens, channels), F32),
            pltpu.VMEM(gate.shape, BF16),
            pltpu.VMEM((2 * STATE, channels), BF16),
            pltpu.VMEM((2 * heads, channels), BF16),
            pltpu.VMEM((CHUNK, channels), F32),
            pltpu.VMEM((tokens, channels), BF16),
            pltpu.SemaphoreType.DMA((5, tokens // CHUNK)),
        ],
        compiler_params=pltpu.CompilerParams(vmem_limit_bytes=VMEM_BYTES),
        name="final_part",
    )(entering, norm_gain, *in_hbm(read, fade, rowed, left, right, gate))


def shards(x, weight, gate, write, read, step, decay, skip, norm_gain):
    place = lax.axis_index("ctx")
    turns = x.shape[1] // LANES
    ends, value = end_state(x, weight, write, step, decay)
    received = lax.all_to_all(ends, "ctx", 0, 0)
    decay, ends = lax.optimization_barrier((decay, ends))
    part = turns // 2
    tables, left = first_local(part, write, read, step, decay, skip[:, None], value)
    gains, fades, reach, keys, mix, rowed = tables
    received, left = lax.optimization_barrier((received, left))
    entering = prefix(place[None], received, weight)
    value, entering = lax.optimization_barrier((value, entering))
    entering = lax.all_to_all(entering, "ctx", 0, 0)
    right = second_local(part, turns - part, gains, fades, keys, mix, rowed, value)
    return final_part(entering, norm_gain[None, :], read, reach, rowed, left, right, gate)


def solution(mesh):
    placed = (
        P("ctx", "tp"),
        P(None, "tp"),
        P("ctx", "tp"),
        P("ctx", "tp"),
        P("ctx", "tp"),
        P("tp", "ctx"),
        P("tp", "ctx"),
        P("tp"),
        P("tp"),
    )
    return jax.shard_map(
        shards, mesh=mesh, in_specs=placed, out_specs=P("ctx", "tp"), check_vma=False
    )
```

```python
import functools

import jax
import jax.numpy as jnp
from jax import lax
from jax.experimental import pallas as pl
from jax.experimental.pallas import tpu as pltpu
from jax.sharding import PartitionSpec as P

F32 = jnp.float32
BF16 = jnp.bfloat16
HEAD = 64
STATE = 128
TAPS = 4
CHUNK = 128
LANES = 256
EXTRA = 16
VMEM_BYTES = 24 * 1024 * 1024


def iota(shape, dim):
    return lax.broadcasted_iota(jnp.int32, shape, dim)


def dot(a, b):
    return jnp.dot(a, b, preferred_element_type=F32)


def dot_binary(a, b):
    high = a.astype(BF16)
    rest = a - high.astype(F32)
    middle = rest.astype(BF16)
    low = (rest - middle.astype(F32)).astype(BF16)
    b = b.astype(BF16)
    return dot(jnp.concatenate([high, middle, low], axis=1), jnp.concatenate([b, b, b], axis=0))


def split(value):
    high = value.astype(BF16)
    return high, (value - high.astype(F32)).astype(BF16)


def silu_of_half(half):
    return half * jnp.tanh(half) + half


def encode(value):
    top = jnp.max(jnp.abs(value), axis=0, keepdims=True)
    scale = jnp.maximum(top * 1.00390625, 1e-30).astype(BF16).astype(F32)
    return jnp.exp2(value * (126.0 / scale)).astype(BF16), scale


def decode(code, scale):
    return jnp.log2(code.astype(F32)) * (scale * (1.0 / 126.0))


def stack_chunks(value):
    pieces = value.shape[1] // CHUNK
    return jnp.concatenate([value[:, CHUNK * c : CHUNK * (c + 1)] for c in range(pieces)], axis=0)


def head_spread(heads, channels):
    return (iota((heads, channels), 0) == iota((heads, channels), 1) // HEAD).astype(F32)


def store_tokens(ref, value, heads):
    for c in range(value.shape[0] // heads):
        part = value[heads * c : heads * (c + 1)]
        high = part.astype(BF16).astype(F32)
        both = jnp.concatenate([high, part - high], axis=0)
        ref[CHUNK * c : CHUNK * (c + 1), :] = both.T.astype(BF16)


def conv_half(rows, weight):
    weight = weight * 0.5
    back = pltpu.roll(rows, 1, 0)
    near = rows * weight[3:4] + back * weight[2:3]
    far = rows * weight[1:2] + back * weight[0:1]
    return (near + pltpu.roll(far, 2, 0))[16:]


def conv_silu(stage, part, start, count, weight):
    half = stage[part, pl.ds(start + 8, count)] * weight[3:4]
    for back in range(1, TAPS):
        half = half + stage[part, pl.ds(start + 8 - back, count)] * weight[3 - back : 4 - back]
    return silu_of_half(half)


def end_state_kernel(
    x_hbm, weight_hbm, write_hbm, step_hbm, decay_hbm, out_hbm, value_hbm,
    x_ref, weight_ref, write_ref, step_ref, decay_ref, gains, spread, keys, packed, stage, out_ref, value_ref, sems,
):
    heads, tokens = step_ref.shape
    pieces = tokens // CHUNK
    channels = heads * HEAD
    turns = channels // LANES
    small = [
        pltpu.make_async_copy(source, target, sems.at[turns + i])
        for i, (source, target) in enumerate(
            ((decay_hbm, decay_ref), (step_hbm, step_ref), (write_hbm, write_ref), (weight_hbm, weight_ref))
        )
    ]

    def fetch(turn):
        lanes = pl.ds(pl.multiple_of(turn * LANES, LANES), LANES)
        return pltpu.make_async_copy(x_hbm.at[:, lanes], x_ref.at[:, lanes], sems.at[turn])

    def leave(turn):
        lanes = pl.ds(pl.multiple_of(turn * LANES, LANES), LANES)
        return pltpu.make_async_copy(
            value_ref.at[turn], value_hbm.at[:, lanes], sems.at[2 * turns + 4 + turn]
        )

    def leave_code(turn):
        places = pl.ds(turn * (LANES // 128), LANES // 128)
        return pltpu.make_async_copy(out_ref.at[places], out_hbm.at[places], sems.at[turns + 4 + turn])

    for copy in small:
        copy.start()
    for turn in range(turns):
        fetch(turn).start()
    ones = head_spread(heads, channels)
    spread[...] = jnp.concatenate([ones, ones], axis=0).astype(BF16)
    for part in range(LANES // 128):
        stage[part, 0:8] = jnp.zeros((8, 128), F32)
    small[0].wait()
    small[1].wait()
    decay = decay_ref[...]
    logs = stack_chunks(decay)
    later = (iota((CHUNK, CHUNK), 0) > iota((CHUNK, CHUNK), 1)).astype(F32)
    suffix = dot_binary(logs, later)
    total = suffix[:, 0:1] + logs[:, 0:1]
    offset = jnp.zeros((heads, 1), F32)
    offsets = []
    for c in reversed(range(pieces)):
        offsets.append(offset)
        offset = offset + total[heads * c : heads * (c + 1)]
    suffix = suffix + jnp.concatenate(offsets[::-1], axis=0)
    gain = jnp.exp(suffix) * stack_chunks(step_ref[...])
    row, lane = (iota(gain.shape, 0), iota(gain.shape, 1))
    gain = jnp.where((row < heads) & (lane < TAPS - 1), 0.0, gain)
    store_tokens(gains, gain, heads)
    first = decay[:, 0:CHUNK]
    lane = iota(first.shape, 1)
    run0 = first[:, 0:1]
    run1 = run0 + first[:, 1:2]
    run2 = run1 + first[:, 2:3]
    step = step_ref[:, 0:CHUNK]
    scalars = jnp.where(lane == 0, jnp.exp(offset), 0.0)
    for t, run in enumerate((run0, run1, run2)):
        scalars = jnp.where(lane == t + 1, jnp.exp(-run) * step[:, t : t + 1], scalars)
    wide = dot_binary(scalars.T[0:8], ones)
    segment = (iota(wide.shape, 1) % HEAD) // (HEAD // 4)
    packed[...] = jnp.broadcast_to(
        jnp.sum(jnp.where(iota(wide.shape, 0) == segment, wide, 0.0), axis=0, keepdims=True),
        packed.shape,
    )
    small[2].wait()
    small[3].wait()
    write_t = write_ref[...].T
    for c in range(pieces):
        part = write_t[:, CHUNK * c : CHUNK * (c + 1)]
        keys[CHUNK * c : CHUNK * (c + 1)] = jnp.concatenate([part, part], axis=1)

    def weigh(turn):
        lanes = pl.ds(pl.multiple_of(turn * LANES, LANES), LANES)
        fetch(turn).wait()
        weight = weight_ref[:, lanes] * 0.5
        state = jnp.zeros((STATE, LANES), F32)
        held = []
        for c in range(pieces):
            span = slice(CHUNK * c, CHUNK * (c + 1))
            rows = x_ref[span, lanes].astype(F32)
            gain = dot(gains[span], spread[:, lanes])
            sides = []
            for part in range(LANES // 128):
                cols = slice(128 * part, 128 * (part + 1))
                stage[part, 8 + CHUNK * c : 8 + CHUNK * (c + 1)] = rows[:, cols]
                value = conv_silu(stage, part, CHUNK * c, CHUNK, weight[:, cols])
                value_ref[turn, span, cols] = value
                sides.append(jnp.concatenate(split(value * gain[:, cols]), axis=0))
            held.append((keys[span], jnp.concatenate(sides, axis=1)))
            if len(held) == 2:
                left, right = zip(*held, strict=True)
                part = dot(jnp.concatenate(left, axis=1), jnp.concatenate(right, axis=0))
                state = part if c < 2 else state + part
                held = []
        leave(turn).start()
        return state

    def finish(turn, state):
        lanes = pl.ds(pl.multiple_of(turn * LANES, LANES), LANES)
        code, scale = encode(state)
        row = iota((EXTRA, LANES), 0)
        first = pltpu.roll(x_ref[0:16, lanes].astype(F32), 7, 0)
        last = pltpu.roll(x_ref[tokens - 16 : tokens, lanes].astype(F32), 7, 0)
        writes = pltpu.roll(write_ref[0:16].astype(F32), 1, 0)
        writes = jnp.concatenate([writes] * (LANES // STATE), axis=1)
        scalar = packed[0:1, lanes]
        high = scalar.astype(BF16).astype(F32)
        middle = (scalar - high).astype(BF16).astype(F32)
        low = scalar - high - middle
        extra = jnp.where(row == 0, scale, 0.0)
        extra = jnp.where((row >= 1) & (row <= 3), writes, extra)
        extra = jnp.where((row >= 4) & (row <= 6), last, extra)
        extra = jnp.where((row >= 7) & (row <= 9), first, extra)
        extra = jnp.where(row == 10, high, extra)
        extra = jnp.where(row == 11, middle, extra)
        extra = jnp.where(row == 12, low, extra).astype(BF16)
        for part in range(LANES // 128):
            place = turn * (LANES // 128) + part
            out_ref[place, 0:STATE] = code[:, 128 * part : 128 * (part + 1)]
            out_ref[place, STATE : STATE + EXTRA] = extra[:, 128 * part : 128 * (part + 1)]

    def pair(i, carry):
        for side in range(2):
            turn = 2 * i + side
            finish(turn, weigh(turn))
            leave_code(turn).start()
        return carry

    lax.fori_loop(0, turns // 2, pair, 0)
    for turn in range(turns):
        leave(turn).wait()
        leave_code(turn).wait()


def in_hbm(*values):
    return [pltpu.with_memory_space_constraint(value, pltpu.HBM) for value in values]


def end_state(x, weight, write, step, decay):
    tokens, channels = x.shape
    heads = step.shape[0]
    owners = channels // 128
    return pl.pallas_call(
        end_state_kernel,
        in_specs=[pl.BlockSpec(memory_space=pltpu.HBM)] * 5,
        out_specs=[pl.BlockSpec(memory_space=pltpu.HBM)] * 2,
        out_shape=[pltpu.HBM((owners, STATE + EXTRA, 128), BF16), pltpu.HBM((tokens, channels), F32)],
        scratch_shapes=[
            pltpu.VMEM(x.shape, BF16),
            pltpu.VMEM(weight.shape, F32),
            pltpu.VMEM(write.shape, BF16),
            pltpu.VMEM(step.shape, F32),
            pltpu.VMEM(decay.shape, F32),
            pltpu.VMEM((tokens, 2 * heads), BF16),
            pltpu.VMEM((2 * heads, channels), BF16),
            pltpu.VMEM((tokens, 2 * CHUNK), BF16),
            pltpu.VMEM((8, channels), F32),
            pltpu.VMEM((LANES // 128, 8 + tokens, 128), F32),
            pltpu.VMEM((owners, STATE + EXTRA, 128), BF16),
            pltpu.VMEM((channels // LANES, tokens, LANES), F32),
            pltpu.SemaphoreType.DMA((3 * (channels // LANES) + 4,)),
        ],
        compiler_params=pltpu.CompilerParams(vmem_limit_bytes=VMEM_BYTES),
        name="end_state",
    )(*in_hbm(x, weight, write, step, decay))


def prefix_kernel(place_ref, in_ref, weight_ref, out_ref, blocks):
    count = in_ref.shape[0]
    tile = in_ref[:, STATE : STATE + EXTRA, :].astype(F32)
    shape = tile.shape
    row, lane = (iota(shape, 1), iota(shape, 2))
    before = jnp.concatenate([jnp.zeros((1,) + shape[1:], F32), tile[:-1]], axis=0)
    rows = jnp.where(
        (row >= 4) & (row <= 6), before, jnp.where((row >= 7) & (row <= 9), tile, 0.0)
    )
    weight = weight_ref[:, pl.ds(pl.multiple_of(place_ref[0] * 128, 128), 128)] * 0.5
    half = rows * weight[3:4][None]
    for back in range(1, TAPS):
        half = half + pltpu.roll(rows, back, 1) * weight[3 - back : 4 - back][None]
    value = silu_of_half(half)
    scalars = jnp.sum(jnp.where((row >= 10) & (row <= 12), tile, 0.0), axis=1, keepdims=True)
    left = iota(scalars.shape, 2) < HEAD

    def spread_of(segment):
        place = segment * (HEAD // 4)
        return jnp.where(
            left, scalars[:, :, place : place + 1], scalars[:, :, HEAD + place : HEAD + place + 1]
        )

    fade = spread_of(0)
    gain = jnp.where(row == 7, spread_of(1), jnp.where(row == 8, spread_of(2), spread_of(3)))
    coarse = value.astype(BF16).astype(F32)
    firsts = jnp.where(row <= 3, pltpu.roll(coarse, EXTRA - 6, 1), pltpu.roll(value - coarse, EXTRA - 3, 1))
    value = jnp.where((row >= 7) & (row <= 9), value * gain, 0.0)
    value = pltpu.roll(value, EXTRA - 6, 1)
    high = value.astype(BF16)
    low = (value - high.astype(F32)).astype(BF16)
    keys = jnp.where((row >= 1) & (row <= 3), tile, 0.0).reshape(count * EXTRA, 128).T.astype(BF16)
    blocks[...] = jnp.zeros(blocks.shape, BF16)
    half = count // 2
    depth = half * EXTRA
    for j in range(count):
        side, place = divmod(j, half)
        lanes = slice(128 * place, 128 * (place + 1))
        start = 2 * depth * side + EXTRA * place
        blocks[start : start + EXTRA, lanes] = high[j]
        blocks[start + depth : start + depth + EXTRA, lanes] = low[j]
    firsts_of = []
    for side in range(2):
        part = keys[:, depth * side : depth * (side + 1)]
        both = blocks[2 * depth * side : 2 * depth * (side + 1)]
        firsts_of.append(dot(jnp.concatenate([part, part], axis=1), both))
    first = jnp.concatenate(firsts_of, axis=1)
    state = jnp.zeros((STATE, 128), F32)
    top_row = iota((EXTRA, 128), 0) == 0
    for j in range(count):
        state = state + first[:, 128 * j : 128 * (j + 1)]
        code, scale = encode(state)
        out_ref[j, 0:STATE] = code
        out_ref[j, STATE : STATE + EXTRA] = jnp.where(top_row, scale, firsts[j]).astype(BF16)
        local = decode(in_ref[j, 0:STATE], tile[j, 0:1])
        state = fade[j] * state + local


def prefix(place, received, weight):
    count = received.shape[0]
    whole = pl.BlockSpec(memory_space=pltpu.VMEM)
    return pl.pallas_call(
        prefix_kernel,
        in_specs=[pl.BlockSpec(memory_space=pltpu.SMEM), whole, whole],
        out_specs=whole,
        out_shape=jax.ShapeDtypeStruct(received.shape, BF16),
        scratch_shapes=[pltpu.VMEM((2 * count * EXTRA, (count // 2) * 128), BF16)],
        compiler_params=pltpu.CompilerParams(vmem_limit_bytes=VMEM_BYTES),
        name="prefix",
    )(place, received, weight)


def make_tables(
    write_ref, read_ref, step_ref, decay_ref, skip_ref, gains, fades, reach, keys, mix, rowed
):
    heads, tokens = step_ref.shape
    pieces = tokens // CHUNK
    channels = heads * HEAD
    ones = head_spread(heads, channels)
    logs = stack_chunks(decay_ref[...])
    upto = (iota((CHUNK, CHUNK), 0) <= iota((CHUNK, CHUNK), 1)).astype(F32)
    run = dot_binary(logs, upto)
    middle = run[:, CHUNK // 2 - 1 : CHUNK // 2]
    total = run[:, CHUNK - 1 : CHUNK]
    gain = jnp.exp(middle - run) * stack_chunks(step_ref[...])
    gain = jnp.where((iota(gain.shape, 0) < heads) & (iota(gain.shape, 1) < TAPS - 1), 0.0, gain)
    store_tokens(gains, gain, heads)
    store_tokens(fades, jnp.exp(run - middle), heads)
    lane = iota((heads, 128), 1)
    scalars = jnp.where(lane == pieces, skip_ref[...], 0.0)
    offset = jnp.zeros((heads, 1), F32)
    offsets = []
    for c in range(pieces):
        offsets.append(offset)
        mid = middle[heads * c : heads * (c + 1)]
        tot = total[heads * c : heads * (c + 1)]
        offset = offset + tot
        if c + 1 < pieces:
            onward = jnp.exp(middle[heads * (c + 1) : heads * (c + 2)] + (tot - mid))
            scalars = jnp.where(lane == c, onward, scalars)
    store_tokens(reach, jnp.exp(run + jnp.concatenate(offsets, axis=0)), heads)
    causal = iota((CHUNK, CHUNK), 0) >= iota((CHUNK, CHUNK), 1)
    for c in range(pieces):
        span = slice(CHUNK * c, CHUNK * (c + 1))
        write = write_ref[span]
        read = read_ref[span]
        mixing = lax.dot_general(read, write, (((1,), (1,)), ((), ())), preferred_element_type=F32)
        if c == 0:
            place = pieces + 1
            for t, later in ((0, 1), (0, 2), (1, 2)):
                weight = jnp.exp(run[0:heads, t : t + 1] - run[0:heads, later : later + 1])
                weight = weight * step_ref[:, later : later + 1] * mixing[t : t + 1, later : later + 1]
                scalars = jnp.where(lane == place, weight, scalars)
                place += 1
        high, low = split(jnp.where(causal, mixing, 0.0))
        mix[span] = jnp.concatenate([high, high, low, read, read], axis=1)
        write_t = write.astype(F32).T.astype(BF16)
        keys[span] = jnp.concatenate([write_t, write_t], axis=1)
    rowed[...] = dot_binary(scalars.T[0 : rowed.shape[0]], ones)


def local_slices(
    begin, ready, value_hbm, local_hbm, gains, fades, keys, mix, rowed,
    value_ref, spread, gain0, gain1, fade0, fade1, result, sems,
):
    tokens, width = local_hbm.shape
    pieces = tokens // CHUNK
    channels = rowed.shape[1]
    turns = width // LANES
    wide_gains, wide_fades = (gain0, gain1), (fade0, fade1)

    def columns(turn):
        return pl.ds(pl.multiple_of(turn * LANES, LANES), LANES)

    def fetch(turn):
        return pltpu.make_async_copy(
            value_hbm.at[:, columns(turn + begin)], value_ref.at[turn], sems.at[turn]
        )

    def leave(turn):
        return pltpu.make_async_copy(
            result.at[turn], local_hbm.at[:, columns(turn)], sems.at[turns + turn]
        )

    def widen(turn, side):
        lanes = columns(turn + begin)
        wide_gains[side][...] = dot(gains[...], spread[:, lanes])
        wide_fades[side][...] = dot(fades[...], spread[:, lanes])

    for turn in range(turns):
        fetch(turn).start()
    ones = head_spread(channels // HEAD, channels)
    spread[...] = jnp.concatenate([ones, ones], axis=0).astype(BF16)
    ready()
    widen(0, 0)

    def work(turn, side):
        lanes = columns(turn + begin)
        fetch(turn).wait()
        skip = rowed[pieces : pieces + 1, lanes]
        widen(jnp.minimum(turn + 1, turns - 1), 1 - side)
        state = None
        for c in range(pieces):
            span = slice(CHUNK * c, CHUNK * (c + 1))
            both = jnp.concatenate(split(value_ref[turn, span] * wide_gains[side][span]), axis=0)
            if state is None:
                mixed = dot(mix[span, 0 : 3 * CHUNK], jnp.concatenate([both, both[0:CHUNK]], axis=0))
                state = dot(keys[span], both)
            else:
                high, low = split(state)
                mixed = dot(mix[span], jnp.concatenate([both, both[0:CHUNK], high, low], axis=0))
                if c + 1 < pieces:
                    state = state + dot(keys[span], both)
            if c + 1 < pieces:
                state = state * rowed[c : c + 1, lanes]
            result[turn, span] = mixed * wide_fades[side][span] + skip * value_ref[turn, span]
        leave(turn).start()

    def pair(i, carry):
        for side in range(2):
            work(2 * i + side, side)
        return carry

    lax.fori_loop(0, turns // 2, pair, 0)
    for turn in range(turns):
        leave(turn).wait()


def first_kernel(
    begin, write_hbm, read_hbm, step_hbm, decay_hbm, skip_ref, value_hbm, *refs
):
    outs, local_hbm, ins, tables, rest = refs[0:6], refs[6], refs[7:11], refs[11:17], refs[17:-1]
    sems = refs[-1]
    arrive = [
        pltpu.make_async_copy(source, target, sems.at[i])
        for i, (source, target) in enumerate(
            zip((write_hbm, read_hbm, step_hbm, decay_hbm), ins, strict=True)
        )
    ]
    depart = [
        pltpu.make_async_copy(source, target, sems.at[4 + i])
        for i, (source, target) in enumerate(zip(tables, outs, strict=True))
    ]
    for copy in arrive:
        copy.start()

    def ready():
        for copy in arrive:
            copy.wait()
        make_tables(*ins, skip_ref, *tables)
        for copy in depart:
            copy.start()

    gains, fades, _, keys, mix, rowed = tables
    local_slices(begin, ready, value_hbm, local_hbm, gains, fades, keys, mix, rowed, *rest)
    for copy in depart:
        copy.wait()


def second_kernel(
    begin, gains_hbm, fades_hbm, keys_hbm, mix_hbm, rowed_hbm, value_hbm, local_hbm, *refs
):
    tables, rest, sems = refs[0:5], refs[5:-1], refs[-1]
    arrive = [
        pltpu.make_async_copy(source, target, sems.at[i])
        for i, (source, target) in enumerate(
            zip((gains_hbm, fades_hbm, keys_hbm, mix_hbm, rowed_hbm), tables, strict=True)
        )
    ]
    for copy in arrive:
        copy.start()

    def ready():
        for copy in arrive:
            copy.wait()

    local_slices(begin, ready, value_hbm, local_hbm, *tables, *rest)


def slice_scratch(turns, tokens, channels):
    return [
        pltpu.VMEM((turns, tokens, LANES), F32),
        pltpu.VMEM((2 * (channels // HEAD), channels), BF16),
        pltpu.VMEM((tokens, LANES), F32),
        pltpu.VMEM((tokens, LANES), F32),
        pltpu.VMEM((tokens, LANES), F32),
        pltpu.VMEM((tokens, LANES), F32),
        pltpu.VMEM((turns, tokens, LANES), F32),
        pltpu.SemaphoreType.DMA((2 * turns,)),
    ]


def first_local(turns, write, read, step, decay, skip, value):
    heads, tokens = step.shape
    pieces = tokens // CHUNK
    channels = heads * HEAD
    hbm = pl.BlockSpec(memory_space=pltpu.HBM)
    tables = [
        ((tokens, 2 * heads), BF16),
        ((tokens, 2 * heads), BF16),
        ((tokens, 2 * heads), BF16),
        ((tokens, 2 * CHUNK), BF16),
        ((tokens, 5 * CHUNK), BF16),
        ((pieces + 8, channels), F32),
    ]
    ins = (write, read, step, decay)
    *out, local = pl.pallas_call(
        functools.partial(first_kernel, 0),
        in_specs=[hbm] * 4 + [pl.BlockSpec(memory_space=pltpu.VMEM), hbm],
        out_specs=[hbm] * 7,
        out_shape=[pltpu.HBM(*table) for table in tables]
        + [pltpu.HBM((tokens, turns * LANES), F32)],
        scratch_shapes=[pltpu.VMEM(source.shape, source.dtype) for source in ins]
        + [pltpu.VMEM(*table) for table in tables]
        + slice_scratch(turns, tokens, channels)
        + [pltpu.SemaphoreType.DMA((len(ins) + len(tables),))],
        compiler_params=pltpu.CompilerParams(vmem_limit_bytes=VMEM_BYTES),
        name="first_local",
    )(*in_hbm(*ins), skip, *in_hbm(value))
    return out, local


def second_local(begin, turns, gains, fades, keys, mix, rowed, value):
    tokens, channels = value.shape
    hbm = pl.BlockSpec(memory_space=pltpu.HBM)
    tables = (gains, fades, keys, mix, rowed)
    return pl.pallas_call(
        functools.partial(second_kernel, begin),
        in_specs=[hbm] * 6,
        out_specs=hbm,
        out_shape=pltpu.HBM((tokens, turns * LANES), F32),
        scratch_shapes=[pltpu.VMEM(table.shape, table.dtype) for table in tables]
        + slice_scratch(turns, tokens, channels)
        + [pltpu.SemaphoreType.DMA((len(tables),))],
        compiler_params=pltpu.CompilerParams(vmem_limit_bytes=VMEM_BYTES),
        name="second_local",
    )(*in_hbm(*tables, value))


def final_kernel(
    state_ref, gain_ref, read_hbm, fade_hbm, rowed_hbm, left_hbm, right_hbm, gate_hbm, out_hbm,
    read_ref, fade_ref, rowed, local_ref, gate_ref, states, spread, gated, out_ref, sems,
):
    owners = state_ref.shape[0]
    channels = owners * 128
    tokens = read_ref.shape[0]
    heads = channels // HEAD
    turns = tokens // CHUNK

    def rows(turn):
        return pl.ds(pl.multiple_of(turn * CHUNK, CHUNK), CHUNK)

    def fetch(turn):
        half = left_hbm.shape[1]
        moves = (
            (left_hbm.at[rows(turn)], local_ref.at[rows(turn), 0:half]),
            (right_hbm.at[rows(turn)], local_ref.at[rows(turn), half:channels]),
            (gate_hbm.at[rows(turn)], gate_ref.at[rows(turn)]),
        )
        return [
            pltpu.make_async_copy(source, target, sems.at[i, turn])
            for i, (source, target) in enumerate(moves)
        ]

    def leave(turn):
        return pltpu.make_async_copy(out_ref.at[rows(turn)], out_hbm.at[rows(turn)], sems.at[4, turn])

    small = [
        pltpu.make_async_copy(read_hbm, read_ref, sems.at[3, 2]),
        pltpu.make_async_copy(fade_hbm, fade_ref, sems.at[3, 3]),
        pltpu.make_async_copy(rowed_hbm, rowed, sems.at[3, 4]),
    ]
    for copy in small:
        copy.start()
    for turn in range(turns):
        for copy in fetch(turn):
            copy.start()
    ones = head_spread(heads, channels)
    spread[...] = jnp.concatenate([ones, ones], axis=0).astype(BF16)
    for k in range(owners):
        value = decode(state_ref[k, 0:STATE], state_ref[k, STATE : STATE + 1].astype(F32))
        high, low = split(value)
        states[0:STATE, 128 * k : 128 * (k + 1)] = high
        states[STATE : 2 * STATE, 128 * k : 128 * (k + 1)] = low
    for copy in small:
        copy.wait()
    for copy in fetch(0):
        copy.wait()
    pieces = tokens // CHUNK
    row = iota((8, 128), 0)
    for k in range(owners):
        lanes = slice(128 * k, 128 * (k + 1))
        firsts = state_ref[k, STATE : STATE + EXTRA].astype(F32)
        value0, value1, value2 = (firsts[t : t + 1] + firsts[t + 3 : t + 4] for t in (1, 2, 3))
        skip, mix01, mix02, mix12 = (rowed[pieces + i : pieces + i + 1, lanes] for i in range(4))
        patch = jnp.where(row == 2, skip * value2, local_ref[0:8, lanes])
        patch = jnp.where(row == 1, skip * value1 - mix12 * value2, patch)
        patch = jnp.where(row == 0, skip * value0 - mix01 * value1 - mix02 * value2, patch)
        local_ref[0:8, lanes] = patch

    def work(turn):
        span = rows(turn)
        read = read_ref[span]
        both = jnp.concatenate([read, read], axis=1)
        fade = fade_ref[span]
        squares = jnp.zeros((CHUNK, 128), F32)
        for j in range(channels // LANES):
            lanes = slice(LANES * j, LANES * (j + 1))
            reach = dot(both, states[:, lanes]) * dot(fade, spread[:, lanes])
            opened = silu_of_half((gate_ref[span, lanes] * 0.5).astype(F32))
            part = (local_ref[span, lanes] + reach) * opened
            gated[:, lanes] = part
            for i in range(LANES // 128):
                piece = part[:, 128 * i : 128 * (i + 1)]
                squares = squares + piece * piece
        inverse = lax.rsqrt(jnp.sum(squares, axis=1, keepdims=True) * (1.0 / channels) + 1e-05)
        for j in range(channels // LANES):
            lanes = slice(LANES * j, LANES * (j + 1))
            out_ref[span, lanes] = (gated[:, lanes] * inverse * gain_ref[:, lanes]).astype(BF16)
        leave(turn).start()

    work(0)

    def later(turn, carry):
        for copy in fetch(turn):
            copy.wait()
        work(turn)
        return carry

    lax.fori_loop(1, turns, later, 0)
    for turn in range(turns):
        leave(turn).wait()


def final_part(entering, norm_gain, read, fade, rowed, left, right, gate):
    tokens, channels = gate.shape
    heads = channels // HEAD
    hbm = pl.BlockSpec(memory_space=pltpu.HBM)
    vmem = pl.BlockSpec(memory_space=pltpu.VMEM)
    return pl.pallas_call(
        final_kernel,
        in_specs=[vmem] * 2 + [hbm] * 6,
        out_specs=hbm,
        out_shape=pltpu.HBM((tokens, channels), BF16),
        scratch_shapes=[
            pltpu.VMEM(read.shape, BF16),
            pltpu.VMEM(fade.shape, BF16),
            pltpu.VMEM(rowed.shape, F32),
            pltpu.VMEM((tokens, channels), F32),
            pltpu.VMEM(gate.shape, BF16),
            pltpu.VMEM((2 * STATE, channels), BF16),
            pltpu.VMEM((2 * heads, channels), BF16),
            pltpu.VMEM((CHUNK, channels), F32),
            pltpu.VMEM((tokens, channels), BF16),
            pltpu.SemaphoreType.DMA((5, tokens // CHUNK)),
        ],
        compiler_params=pltpu.CompilerParams(vmem_limit_bytes=VMEM_BYTES),
        name="final_part",
    )(entering, norm_gain, *in_hbm(read, fade, rowed, left, right, gate))


def shards(x, weight, gate, write, read, step, decay, skip, norm_gain):
    place = lax.axis_index("ctx")
    turns = x.shape[1] // LANES
    ends, value = end_state(x, weight, write, step, decay)
    received = lax.all_to_all(ends, "ctx", 0, 0)
    decay, ends = lax.optimization_barrier((decay, ends))
    part = turns // 2
    tables, left = first_local(part, write, read, step, decay, skip[:, None], value)
    gains, fades, reach, keys, mix, rowed = tables
    received, left = lax.optimization_barrier((received, left))
    entering = prefix(place[None], received, weight)
    value, entering = lax.optimization_barrier((value, entering))
    entering = lax.all_to_all(entering, "ctx", 0, 0)
    right = second_local(part, turns - part, gains, fades, keys, mix, rowed, value)
    return final_part(entering, norm_gain[None, :], read, reach, rowed, left, right, gate)


def solution(mesh):
    placed = (
        P("ctx", "tp"),
        P(None, "tp"),
        P("ctx", "tp"),
        P("ctx", "tp"),
        P("ctx", "tp"),
        P("tp", "ctx"),
        P("tp", "ctx"),
        P("tp"),
        P("tp"),
    )
    return jax.shard_map(
        shards, mesh=mesh, in_specs=placed, out_specs=P("ctx", "tp"), check_vma=False
    )
```
